128 devices in a mesh: req: 4 (over y), ctx: 32 (over z, x, core).
Axes of the slice: x: 4, y: 4, z: 4, core: 2. Of those that a mesh axis runs over, the one named last changes fastest.
Arguments:
- queries: bfloat16 [16384, 8192], P(('req', 'ctx')), parts along dimension 0, may hold values from -10 to 10
- keys: bfloat16 [131072, 1024], P(('req', 'ctx')), parts along dimension 0, may hold values from -5 to 5
- values: bfloat16 [131072, 1024], P(('req', 'ctx')), parts along dimension 0, may hold values from -6 to 6
- lengths: int32 [128], P(('req', 'ctx')), parts along dimension 0, may hold values from 128 to 1024, as said below
- owner: int32 [4], P('req'), parts along dimension 0, may hold values from 0 to 31
Outputs:
- attended: bfloat16 [512, 8192], P('req', 'ctx'), parts along dimension 0
The draws below stay inside these ranges and needn't reach their ends.
There are 4 independent parts, one for each index of `req`. The reference program is written for one: setup_inputs(seed, part) draws one part's arguments, and reference() takes and returns one part's arrays. A program takes and returns all parts, laid end to end along the dimension named above; each array names one. Nothing has to cross between parts.
Inputs may be any that keep to these rules, and one draw needn't show every extreme that they name: `lengths`: multiples of 128; some block holds 1024 valid positions.
All inputs are finite; a program needn't handle non-finite values.
Results may differ from the reference program's by a relative error of at most 0.0028.
Values may be sent and summed in bfloat16 or wider, within the bound.
A program may use at most 320 MiB of HBM per device.

```python
import jax
import jax.numpy as jnp
from jax import lax

H = 64
KVH = 8
DH = 128
Q = 128
BLK = 1024
NBLK = 32


def draw_queries(key, part):
    key = jax.random.fold_in(key, 3)
    base = jnp.clip(2.5 * jax.random.normal(key, (NBLK * Q, H * DH), jnp.float32), -10.0, 10.0)
    return base.astype(jnp.bfloat16)


def draw_keys(key, part):
    key = jax.random.fold_in(key, 4)
    base = jnp.clip(jax.random.normal(key, (NBLK * BLK, KVH * DH), jnp.float32), -5.0, 5.0)
    return base.astype(jnp.bfloat16)


def draw_lengths(key, part):
    key = jax.random.fold_in(key, 5)
    first_key, second_key = jax.random.split(key)
    counts = 128 * jax.random.randint(first_key, (NBLK,), 1, BLK // 128 + 1, dtype=jnp.int32)
    full_block = jax.random.randint(second_key, (), 0, NBLK, dtype=jnp.int32)
    return jnp.where(jnp.arange(NBLK, dtype=jnp.int32) == full_block, BLK, counts).astype(jnp.int32)


def levels(key, dims, cuts, low, largest):
    def one(axis_at, shards_of):
        steps = jax.random.uniform(jax.random.fold_in(jax.random.fold_in(key, 6), axis_at), (shards_of,), jnp.float32, low / len(cuts), largest / len(cuts))
        return jnp.repeat(jnp.exp(steps), dims[axis_at] // shards_of).reshape((-1,) + (1,) * (len(dims) - axis_at - 1))

    level = one(*cuts[0])
    for cut in cuts[1:]:
        level = level * one(*cut)
    return level


def gaussian(stream_key, extent, width, reach, cuts=(), kind=jnp.bfloat16):
    drawn = width * jax.random.normal(stream_key, extent, jnp.float32)
    if cuts:
        drawn = drawn * levels(stream_key, extent, cuts, -0.22, 0.18)
    return jnp.clip(drawn, -reach, reach).astype(kind)


def setup_inputs(seed: int = 0, part: int = 0) -> dict:
    splits = jax.random.split(jax.random.key(seed), 6)
    own_keys = jax.random.split(jax.random.fold_in(splits[5], part), 6)
    return {
        "queries": draw_queries(jax.random.fold_in(jax.random.fold_in(splits[5], part), 71), part),
        "keys": draw_keys(jax.random.fold_in(jax.random.fold_in(splits[5], part), 71), part),
        "values": gaussian(own_keys[2], (NBLK * BLK, KVH * DH), 1.0, 6.0, ((0, 32),)),
        "lengths": draw_lengths(jax.random.fold_in(jax.random.fold_in(splits[5], part), 71), part),
        "owner": jax.random.randint(own_keys[4], (1,), 0, NBLK).astype(jnp.int32),
    }


def block_partial(query_heads, keys, values, lengths, index):
    start = (index * BLK).astype(jnp.int32)
    key_rows = lax.dynamic_slice_in_dim(keys, start, BLK, 0).astype(jnp.float32).reshape(BLK, KVH, DH)
    value_rows = lax.dynamic_slice_in_dim(values, start, BLK, 0).astype(jnp.float32).reshape(BLK, KVH, DH)
    scores = jnp.einsum("qkgd,tkd->kgqt", query_heads, key_rows) * (DH ** -0.5)
    valid_keys = jnp.arange(BLK, dtype=jnp.int32) < lengths[index]
    scores = jnp.where(valid_keys, scores, -jnp.inf)
    highest = jnp.max(scores, axis=-1)
    weights = jnp.exp(scores - highest[..., None])
    totals = jnp.sum(weights, axis=-1)
    rounded = lax.optimization_barrier(weights.astype(jnp.bfloat16)).astype(jnp.float32)
    partial_value = jnp.einsum("kgqt,tkd->qkgd", rounded, value_rows) / jnp.transpose(totals, (2, 0, 1))[..., None]
    log_total = jnp.transpose(highest + jnp.log(totals), (2, 0, 1))
    return partial_value.reshape(Q, H * DH), log_total.reshape(Q, H)


def reference(queries, keys, values, lengths, owner):
    owner_row = (owner[0] * Q).astype(jnp.int32)
    query_heads = lax.dynamic_slice_in_dim(queries, owner_row, Q, 0).astype(jnp.float32).reshape(Q, KVH, H // KVH, DH)

    def one_block(index):
        return block_partial(query_heads, keys, values, lengths, index)

    partials, log_totals = lax.map(one_block, jnp.arange(NBLK, dtype=jnp.int32))
    highest = jnp.max(log_totals, axis=0)
    overall = highest + jnp.log(jnp.sum(jnp.exp(log_totals - highest), axis=0))
    factors = jnp.exp(log_totals - overall)
    merged = jnp.sum(factors[..., None] * partials.reshape(NBLK, Q, H, DH), axis=0)
    return merged.reshape(Q, H * DH).astype(jnp.bfloat16)
```

```python
import functools
import math

import jax
import jax.numpy as jnp
from jax import lax
from jax.experimental import pallas as pl
from jax.experimental.pallas import tpu as pltpu
from jax.sharding import PartitionSpec as P

H = 64
KVH = 8
DH = 128
Q = 128
BLK = 1024
GROUP = H // KVH
HALF = H * DH // 2
KV_HALF = KVH // 2
SIDE = 4
QUARTER = HALF // 2 // SIDE
ROWS = 32
CHUNKS = Q // ROWS
SCALE = DH**-0.5 * math.log2(math.e)
MESH = pl.DeviceIdType.MESH
HOPS = (2, 1, 3)
AB = (((1,), (0,)), ((), ()))


def pick(index, parts):
    out = parts[-1]
    for i in range(len(parts) - 2, -1, -1):
        out = jnp.where(index == i, parts[i], out)
    return out


def kernel(
    lengths_ref, owner_ref, queries_ref, keys_ref, values_ref, out_ref,
    cand, s1, r1, r2, qf, kraw, vraw, lens, kt, va, c1, c1l, g1, g1l, c2, g2,
    core_send, core_recv, kv_send, kv_recv, own_sem,
    q_send, q_recv, c1_send, c1_recv, c2_send, c2_recv,
):
    req = lax.axis_index("req")
    me = lax.axis_index("ctx")
    c = lax.rem(me, 2)
    x = lax.rem(me // 2, SIDE)
    z = me // (2 * SIDE)
    owner = owner_ref[0]
    owner_c = lax.rem(owner, 2)
    owner_x = lax.rem(owner // 2, SIDE)
    owner_z = owner // (2 * SIDE)

    def device(zz, xx, cc):
        return (req, (zz * SIDE + xx) * 2 + cc)

    def along_x(k):
        return lax.rem(x + k, SIDE)

    def along_z(k):
        return lax.rem(z + k, SIDE)

    sibling = device(z, x, 1 - c)

    def remote(src, dst, send, recv, to):
        return pltpu.make_async_remote_copy(
            src_ref=src, dst_ref=dst, send_sem=send, recv_sem=recv, device_id=to, device_id_type=MESH
        )

    barrier = pltpu.get_barrier_semaphore()
    peers = [sibling]
    for k in (1, 2, 3):
        peers += [device(z, along_x(k), c), device(along_z(k), x, 0), device(along_z(k), x, 1)]
    for to in peers:
        pl.semaphore_signal(barrier, inc=1, device_id=to, device_id_type=MESH)

    own_cols = pl.ds(pl.multiple_of(c * HALF, HALF), HALF)
    sib_cols = pl.ds(pl.multiple_of((1 - c) * HALF, HALF), HALF)
    kv_width = KV_HALF * DH
    own_kv = pl.ds(pl.multiple_of(c * kv_width, kv_width), kv_width)
    sib_kv = pl.ds(pl.multiple_of((1 - c) * kv_width, kv_width), kv_width)

    own = [
        pltpu.make_async_copy(
            queries_ref.at[pl.ds(ch * ROWS, ROWS), own_cols], cand.at[ch, c], own_sem.at[ch]
        )
        for ch in range(CHUNKS)
    ]
    own_k = pltpu.make_async_copy(keys_ref.at[:, own_kv], kraw.at[c], own_sem.at[CHUNKS])
    own_v = pltpu.make_async_copy(values_ref.at[:, own_kv], vraw.at[c], own_sem.at[CHUNKS + 1])
    for copy in own + [own_k, own_v]:
        copy.start()
    lens[c] = jnp.full((8, 128), lengths_ref[0], jnp.int32)

    pl.semaphore_wait(barrier, len(peers))

    core_q = [
        remote(
            queries_ref.at[pl.ds(ch * ROWS, ROWS), sib_cols], cand.at[ch, c],
            core_send.at[ch], core_recv.at[ch], sibling,
        )
        for ch in range(CHUNKS)
    ]
    core_kv = [
        remote(lens.at[c], lens.at[c], kv_send.at[0], kv_recv.at[0], sibling),
        remote(keys_ref.at[:, sib_kv], kraw.at[c], kv_send.at[1], kv_recv.at[1], sibling),
        remote(values_ref.at[:, sib_kv], vraw.at[c], kv_send.at[2], kv_recv.at[2], sibling),
    ]
    for copy in core_q + core_kv:
        copy.start()

    def quarter(index, half):
        return pl.ds(pl.multiple_of(half * (HALF // 2) + index * QUARTER, QUARTER), QUARTER)

    def spread_copies(ch, stage):
        copies = []
        for i, k in enumerate(HOPS):
            for half in range(2):
                on_x = (stage + half) % 2 == 0
                to = device(z, along_x(k), c) if on_x else device(along_z(k), x, c)
                peer = along_x(k) if on_x else along_z(k)
                here = x if on_x else z
                if stage == 0:
                    src, dst = s1.at[ch, :, quarter(peer, half)], r1.at[ch, half, here]
                elif stage == 1:
                    src = dst = r2.at[ch, half, here]
                else:
                    src = dst = qf.at[ch, :, quarter(here, half)]
                copies.append(
                    remote(src, dst, q_send.at[ch, stage, half, i], q_recv.at[ch, stage, half, i], to)
                )
        return copies

    for ch in range(CHUNKS):
        own[ch].wait()
        core_q[ch].wait_recv()
        s1[ch] = pick(owner_c, [cand[ch, 0], cand[ch, 1]])
        for copy in spread_copies(ch, 0):
            copy.start()
        r1[ch, 0, x] = s1[ch, :, quarter(x, 0)]
        r1[ch, 1, z] = s1[ch, :, quarter(z, 1)]

    def prepare(block):
        valid = lax.broadcasted_iota(jnp.int32, (BLK, DH), 0) < lens[block, 0:1, :]
        ones = jnp.where(valid, 1.0, 0.0).astype(jnp.bfloat16)
        rows = pl.ds(block * BLK, BLK)
        for kv in range(KV_HALF):
            cols = slice(kv * DH, (kv + 1) * DH)
            head = kraw[block, :, cols].astype(jnp.float32)
            head = jnp.where(valid, head, jnp.concatenate([head[:DH]] * (BLK // DH), axis=0)) * SCALE
            high = head.astype(jnp.bfloat16)
            low = (head - high.astype(jnp.float32)).astype(jnp.bfloat16)
            kt[kv, 0:DH, rows] = high.T
            kt[kv, DH : 2 * DH, rows] = low.T
            value = vraw[block, :, cols].astype(jnp.float32)
            va[kv, rows, 0:DH] = jnp.where(valid, value, 0.0).astype(jnp.bfloat16)
            va[kv, rows, DH : 2 * DH] = ones

    own_k.wait()
    own_v.wait()
    for copy in core_kv:
        copy.wait_recv()
    prepare(0)

    for ch in range(CHUNKS):
        for copy in spread_copies(ch, 0):
            copy.wait_recv()
        r2[ch, 0, z] = pick(owner_x, [r1[ch, 0, i] for i in range(SIDE)])
        r2[ch, 1, x] = pick(owner_z, [r1[ch, 1, i] for i in range(SIDE)])
        for copy in spread_copies(ch, 1):
            copy.start()

    prepare(1)

    for ch in range(CHUNKS):
        for copy in spread_copies(ch, 1):
            copy.wait_recv()
        qf[ch, :, quarter(x, 0)] = pick(owner_z, [r2[ch, 0, i] for i in range(SIDE)])
        qf[ch, :, quarter(z, 1)] = pick(owner_x, [r2[ch, 1, i] for i in range(SIDE)])
        for copy in spread_copies(ch, 2):
            copy.start()

    lane = lax.broadcasted_iota(jnp.int32, (ROWS, 128), 1)

    def scores(ch, kv):
        rows = [qf[ch, :, (kv * GROUP + i) * DH : (kv * GROUP + i + 1) * DH] for i in range(GROUP)]
        rows = jnp.concatenate(rows, axis=0)
        rows = jnp.concatenate([rows, rows], axis=1)
        return lax.dot_general(rows, kt[kv], AB, preferred_element_type=jnp.float32)

    def attend(ch, kv, s, logs):
        tops, sums = [], []
        for block in range(2):
            part = s[:, block * BLK : (block + 1) * BLK]
            top = jnp.max(part, axis=1, keepdims=True)
            weights = jnp.exp2(part - top).astype(jnp.bfloat16)
            rows = slice(block * BLK, (block + 1) * BLK)
            sums.append(lax.dot_general(weights, va[kv, rows], AB, preferred_element_type=jnp.float32))
            tops.append(top)
        highest = jnp.maximum(tops[0], tops[1])
        both = jnp.exp2(tops[0] - highest) * sums[0] + jnp.exp2(tops[1] - highest) * sums[1]
        totals = both[:, DH:]
        partial = (both[:, :DH] / totals).astype(jnp.bfloat16)
        log_total = highest + jnp.log2(totals)
        for i in range(GROUP):
            to = (kv % 2) * 2 + i // 4
            place = (kv // 2) * 4 + i % 4
            part = slice(i * ROWS, (i + 1) * ROWS)
            c1[ch, to, :, place * DH : (place + 1) * DH] = partial[part]
            logs[to] = jnp.where(lane == place, log_total[part], logs[to])

    def merge_copies(ch):
        copies = []
        for i, k in enumerate(HOPS):
            peer = along_x(k)
            to = device(z, peer, c)
            copies.append(
                remote(c1.at[ch, peer], g1.at[ch, x], c1_send.at[ch, 0, i], c1_recv.at[ch, 0, i], to)
            )
            copies.append(
                remote(c1l.at[ch, peer], g1l.at[ch, x], c1_send.at[ch, 1, i], c1_recv.at[ch, 1, i], to)
            )
        return copies

    def compute(ch):
        logs = [jnp.zeros((ROWS, 128), jnp.float32) for _ in range(SIDE)]
        s = scores(ch, 0)
        for kv in range(KV_HALF):
            later = scores(ch, kv + 1) if kv + 1 < KV_HALF else None
            attend(ch, kv, s, logs)
            s = later
        for to in range(SIDE):
            c1l[ch, to] = logs[to]
        for copy in merge_copies(ch):
            copy.start()
        g1[ch, x] = c1[ch, x]
        g1l[ch, x] = c1l[ch, x]

    def weigh(parts):
        top = functools.reduce(jnp.maximum, parts)
        factors = [jnp.exp2(part - top) for part in parts]
        total = functools.reduce(jnp.add, factors)
        return [factor / total for factor in factors], top + jnp.log2(total)

    def finals(ch, act):
        for zi in range(2):
            for core in range(2):
                place = zi * 2 + core
                zz = 2 * c + zi
                here = jnp.logical_and(zz == z, core == c)
                copy = remote(
                    c2.at[ch, place], g2.at[ch, z], c2_send.at[ch, place], c2_recv.at[ch, z], device(zz, x, core)
                )
                act(place, here, copy)

    def merge(ch):
        for copy in merge_copies(ch):
            copy.wait_recv()
        factors, logs = weigh([g1l[ch, i] for i in range(SIDE)])
        for head in range(8):
            cols = slice(head * DH, (head + 1) * DH)
            added = functools.reduce(
                jnp.add,
                [factors[i][:, head : head + 1] * g1[ch, i, :, cols].astype(jnp.float32) for i in range(SIDE)],
            )
            c2[ch, head // 2, :, (head % 2) * DH : (head % 2 + 1) * DH] = added
        for place in range(4):
            c2[ch, place, :, 2 * DH :] = logs

        def send(place, here, copy):
            @pl.when(jnp.logical_not(here))
            def _():
                copy.start()

            @pl.when(here)
            def _():
                g2[ch, z] = c2[ch, place]

        finals(ch, send)

    def finish(ch):
        for zz in range(SIDE):
            @pl.when(jnp.logical_or(zz != z, z // 2 != c))
            def _():
                remote(
                    c2.at[ch, 0], g2.at[ch, zz], c2_send.at[ch, 0], c2_recv.at[ch, zz], sibling
                ).wait_recv()

        for idx in range(2):
            mine = lane == lax.rem(z, 2) * 4 + c * 2 + idx
            logs = [
                jnp.sum(jnp.where(mine, g2[ch, i, :, 2 * DH :], 0.0), axis=1, keepdims=True) for i in range(SIDE)
            ]
            factors, _ = weigh(logs)
            cols = slice(idx * DH, (idx + 1) * DH)
            added = functools.reduce(jnp.add, [factors[i] * g2[ch, i, :, cols] for i in range(SIDE)])
            out_ref[ch * ROWS : (ch + 1) * ROWS, cols] = added.astype(jnp.bfloat16)

    for ch in range(CHUNKS):
        for copy in spread_copies(ch, 2):
            copy.wait_recv()
        compute(ch)
        if ch > 0:
            merge(ch - 1)
    merge(CHUNKS - 1)
    for ch in range(CHUNKS):
        finish(ch)

    for copy in core_q + core_kv:
        copy.wait_send()
    for ch in range(CHUNKS):
        for stage in range(3):
            for copy in spread_copies(ch, stage):
                copy.wait_send()
        for copy in merge_copies(ch):
            copy.wait_send()

        def left(place, here, copy):
            @pl.when(jnp.logical_not(here))
            def _():
                copy.wait_send()

        finals(ch, left)


def on_device(queries, keys, values, lengths, owner):
    vmem, dma = pltpu.VMEM, pltpu.SemaphoreType.DMA
    any_space = pl.BlockSpec(memory_space=pl.ANY)
    smem = pl.BlockSpec(memory_space=pltpu.SMEM)
    bf16, f32 = jnp.bfloat16, jnp.float32
    return pl.pallas_call(
        kernel,
        out_shape=jax.ShapeDtypeStruct((Q, 2 * DH), bf16),
        in_specs=[smem, smem, any_space, any_space, any_space],
        out_specs=pl.BlockSpec(memory_space=vmem),
        scratch_shapes=[
            vmem((CHUNKS, 2, ROWS, HALF), bf16),
            vmem((CHUNKS, ROWS, HALF), bf16),
            vmem((CHUNKS, 2, SIDE, ROWS, QUARTER), bf16),
            vmem((CHUNKS, 2, SIDE, ROWS, QUARTER), bf16),
            vmem((CHUNKS, ROWS, HALF), bf16),
            vmem((2, BLK, KV_HALF * DH), bf16),
            vmem((2, BLK, KV_HALF * DH), bf16),
            vmem((2, 8, 128), jnp.int32),
            vmem((KV_HALF, 2 * DH, 2 * BLK), bf16),
            vmem((KV_HALF, 2 * BLK, 2 * DH), bf16),
            vmem((CHUNKS, SIDE, ROWS, 8 * DH), bf16),
            vmem((CHUNKS, SIDE, ROWS, 128), f32),
            vmem((CHUNKS, SIDE, ROWS, 8 * DH), bf16),
            vmem((CHUNKS, SIDE, ROWS, 128), f32),
            vmem((CHUNKS, 4, ROWS, 3 * DH), f32),
            vmem((CHUNKS, SIDE, ROWS, 3 * DH), f32),
            dma((CHUNKS,)), dma((CHUNKS,)),
            dma((3,)), dma((3,)),
            dma((CHUNKS + 2,)),
            dma((CHUNKS, 3, 2, 3)), dma((CHUNKS, 3, 2, 3)),
            dma((CHUNKS, 2, 3)), dma((CHUNKS, 2, 3)),
            dma((CHUNKS, 4)), dma((CHUNKS, SIDE)),
        ],
        compiler_params=pltpu.CompilerParams(
            collective_id=0, has_side_effects=True, vmem_limit_bytes=56 * 2**20
        ),
        cost_estimate=pl.CostEstimate(
            flops=4 * H * Q * BLK * DH, bytes_accessed=6 * 2**20, transcendentals=H * Q * BLK
        ),
    )(lengths, owner, queries, keys, values)


def solution(mesh):
    in_specs = (
        P(("req", "ctx"), None),
        P(("req", "ctx"), None),
        P(("req", "ctx"), None),
        P(("req", "ctx")),
        P("req"),
    )
    return jax.shard_map(
        on_device, mesh=mesh, in_specs=in_specs, out_specs=P("req", "ctx"), check_vma=False
    )
```

```python
import functools
import math

import jax
import jax.numpy as jnp
from jax import lax
from jax.experimental import pallas as pl
from jax.experimental.pallas import tpu as pltpu
from jax.sharding import PartitionSpec as P

H = 64
KVH = 8
DH = 128
Q = 128
BLK = 1024
GROUP = H // KVH
HALF = H * DH // 2
KV_HALF = KVH // 2
SIDE = 4
QUARTER = HALF // 2 // SIDE
ROWS = 32
CHUNKS = Q // ROWS
SCALE = DH**-0.5 * math.log2(math.e)
STEPS = 32000.0
TINY = 1e-30
MESH = pl.DeviceIdType.MESH
HOPS = (2, 1, 3)
AB = (((1,), (0,)), ((), ()))


def pick(index, parts):
    out = parts[-1]
    for i in range(len(parts) - 2, -1, -1):
        out = jnp.where(index == i, parts[i], out)
    return out


def kernel(
    lengths_ref, owner_ref, queries_ref, keys_ref, values_ref, out_ref,
    cand, s1, r1, r2, qf, raw, lens, kt, va,
    ca, sa, cb, sb, ga, gsa, gb, gsb, da, db, ha, hb,
    core_send, core_recv, kv_send, kv_recv, own_sem, q_send, q_recv,
    first_send, first_recv, second_send, second_recv,
):
    req = lax.axis_index("req")
    me = lax.axis_index("ctx")
    c = lax.rem(me, 2)
    x = lax.rem(me // 2, SIDE)
    z = me // (2 * SIDE)
    owner = owner_ref[0]
    owner_c = lax.rem(owner, 2)
    owner_x = lax.rem(owner // 2, SIDE)
    owner_z = owner // (2 * SIDE)

    def device(zz, xx, cc):
        return (req, (zz * SIDE + xx) * 2 + cc)

    def along_x(k):
        return lax.rem(x + k, SIDE)

    def along_z(k):
        return lax.rem(z + k, SIDE)

    sibling = device(z, x, 1 - c)

    def wait(ref, sem):
        pltpu.make_async_copy(ref, ref, sem).wait()

    def remote(src, dst, send, recv, to):
        return pltpu.make_async_remote_copy(
            src_ref=src, dst_ref=dst, send_sem=send, recv_sem=recv, device_id=to, device_id_type=MESH
        )

    barrier = pltpu.get_barrier_semaphore()
    peers = [sibling]
    for k in (1, 2, 3):
        for core in range(2):
            peers += [device(z, along_x(k), core), device(along_z(k), x, core)]
    for to in peers:
        pl.semaphore_signal(barrier, inc=1, device_id=to, device_id_type=MESH)

    own_cols = pl.ds(pl.multiple_of(c * HALF, HALF), HALF)
    sib_cols = pl.ds(pl.multiple_of((1 - c) * HALF, HALF), HALF)
    kv_width = KV_HALF * DH
    own_kv = pl.ds(pl.multiple_of(c * kv_width, kv_width), kv_width)
    sib_kv = pl.ds(pl.multiple_of((1 - c) * kv_width, kv_width), kv_width)

    own = [
        pltpu.make_async_copy(
            queries_ref.at[pl.ds(ch * ROWS, ROWS), own_cols], cand.at[ch, c], own_sem.at[ch]
        )
        for ch in range(CHUNKS)
    ]
    own_k = pltpu.make_async_copy(keys_ref.at[:, own_kv], raw.at[c, 0], own_sem.at[CHUNKS])
    own_v = pltpu.make_async_copy(values_ref.at[:, own_kv], raw.at[c, 1], own_sem.at[CHUNKS + 1])
    for copy in own + [own_k, own_v]:
        copy.start()
    lens[c] = jnp.full((8, 128), lengths_ref[0], jnp.int32)

    pl.semaphore_wait(barrier, len(peers))

    core_q = [
        remote(
            queries_ref.at[pl.ds(ch * ROWS, ROWS), sib_cols], cand.at[ch, c],
            core_send, core_recv.at[ch], sibling,
        )
        for ch in range(CHUNKS)
    ]
    core_kv = [
        remote(lens.at[c], lens.at[c], kv_send.at[0], kv_recv.at[0], sibling),
        remote(keys_ref.at[:, sib_kv], raw.at[c, 0], kv_send.at[1], kv_recv.at[1], sibling),
        remote(values_ref.at[:, sib_kv], raw.at[c, 1], kv_send.at[1], kv_recv.at[1], sibling),
    ]
    for copy in core_q + core_kv:
        copy.start()

    def quarter(index, half):
        return pl.ds(pl.multiple_of(half * (HALF // 2) + index * QUARTER, QUARTER), QUARTER)

    def spread_copies(ch, stage):
        copies = []
        for k in HOPS:
            for half in range(2):
                on_x = (stage + half) % 2 == 0
                to = device(z, along_x(k), c) if on_x else device(along_z(k), x, c)
                peer = along_x(k) if on_x else along_z(k)
                here = x if on_x else z
                if stage == 0:
                    src, dst = s1.at[ch, :, quarter(peer, half)], r1.at[ch, half, here]
                elif stage == 1:
                    src = dst = r2.at[ch, half, here]
                else:
                    src = dst = qf.at[ch, :, quarter(here, half)]
                copies.append(remote(src, dst, q_send.at[stage], q_recv.at[ch, stage], to))
        return copies

    def spread_wait(ch, stage):
        wait(r1.at[ch, :, 0 : SIDE - 1], q_recv.at[ch, stage])

    for ch in range(CHUNKS):
        own[ch].wait()
        core_q[ch].wait_recv()
        s1[ch] = pick(owner_c, [cand[ch, 0], cand[ch, 1]])
        for copy in spread_copies(ch, 0):
            copy.start()
        r1[ch, 0, x] = s1[ch, :, quarter(x, 0)]
        r1[ch, 1, z] = s1[ch, :, quarter(z, 1)]

    def prepare(block):
        valid = lax.broadcasted_iota(jnp.int32, (BLK, DH), 0) < lens[block, 0:1, :]
        ones = jnp.where(valid, 1.0, 0.0).astype(jnp.bfloat16)
        rows = pl.ds(block * BLK, BLK)
        for kv in range(KV_HALF):
            cols = slice(kv * DH, (kv + 1) * DH)
            head = raw[block, 0, :, cols].astype(jnp.float32)
            head = jnp.where(valid, head, jnp.concatenate([head[:DH]] * (BLK // DH), axis=0)) * SCALE
            high = head.astype(jnp.bfloat16)
            low = (head - high.astype(jnp.float32)).astype(jnp.bfloat16)
            kt[kv, 0:DH, rows] = high.T
            kt[kv, DH : 2 * DH, rows] = low.T
            value = raw[block, 1, :, cols].astype(jnp.float32)
            va[kv, rows, 0:DH] = jnp.where(valid, value, 0.0).astype(jnp.bfloat16)
            va[kv, rows, DH : 2 * DH] = ones

    own_k.wait()
    own_v.wait()
    wait(lens.at[0], kv_recv.at[0])
    wait(raw.at[0], kv_recv.at[1])
    prepare(0)

    for ch in range(CHUNKS):
        spread_wait(ch, 0)
        r2[ch, 0, z] = pick(owner_x, [r1[ch, 0, i] for i in range(SIDE)])
        r2[ch, 1, x] = pick(owner_z, [r1[ch, 1, i] for i in range(SIDE)])
        for copy in spread_copies(ch, 1):
            copy.start()

    prepare(1)

    for ch in range(CHUNKS):
        spread_wait(ch, 1)
        qf[ch, :, quarter(x, 0)] = pick(owner_z, [r2[ch, 0, i] for i in range(SIDE)])
        qf[ch, :, quarter(z, 1)] = pick(owner_x, [r2[ch, 1, i] for i in range(SIDE)])
        for copy in spread_copies(ch, 2):
            copy.start()

    diagonal = lax.broadcasted_iota(jnp.int32, (ROWS, 128), 0) == lax.broadcasted_iota(jnp.int32, (ROWS, 128), 1)

    def to_row(wide):
        return jnp.sum(jnp.where(diagonal, wide, 0.0), axis=-2)

    def to_column(row):
        return jnp.sum(jnp.where(diagonal, row, 0.0), axis=1, keepdims=True)

    def scores(ch, kv):
        rows = [qf[ch, :, (kv * GROUP + i) * DH : (kv * GROUP + i + 1) * DH] for i in range(GROUP)]
        rows = jnp.concatenate(rows, axis=0)
        rows = jnp.concatenate([rows, rows], axis=1)
        return lax.dot_general(rows, kt[kv], AB, preferred_element_type=jnp.float32)

    def attend(ch, kv, s):
        tops, sums = [], []
        for block in range(2):
            part = s[:, block * BLK : (block + 1) * BLK]
            top = jnp.max(part, axis=1, keepdims=True)
            weights = jnp.exp2(part - top).astype(jnp.bfloat16)
            rows = slice(block * BLK, (block + 1) * BLK)
            sums.append(lax.dot_general(weights, va[kv, rows], AB, preferred_element_type=jnp.float32))
            tops.append(top)
        highest = jnp.maximum(tops[0], tops[1])
        both = jnp.exp2(tops[0] - highest) * sums[0] + jnp.exp2(tops[1] - highest) * sums[1]
        totals = both[:, DH:]
        largest = jnp.max(jnp.abs(both[:, :DH]), axis=1, keepdims=True)
        largest = jnp.maximum(largest, TINY)
        partial = jnp.round(both[:, :DH] * (STEPS / largest)).astype(jnp.int32).astype(jnp.int16)
        step = largest * (1.0 / STEPS) / totals
        log_total = highest + jnp.log2(totals)
        log_rows = to_row(log_total.reshape(GROUP, ROWS, DH))
        step_rows = to_row(step.reshape(GROUP, ROWS, DH))
        zi = kv // 2
        for i in range(GROUP):
            xx, core = (kv % 2) * 2 + i // 4, (i % 4) // 2
            part = partial[i * ROWS : (i + 1) * ROWS]
            if i % 2 == 0:
                place, to, box, stats, count = zi * 2 + core, xx, ca, sa, 4
            else:
                place, to, box, stats, count = xx * 2 + core, zi, cb, sb, 8
            box[ch, to, :, place * DH : (place + 1) * DH] = part
            stats[ch, to, place : place + 1] = log_rows[i : i + 1]
            stats[ch, to, count + place : count + place + 1] = step_rows[i : i + 1]

    merger = c == z // 2

    def first_copies(ch, act):
        for k in HOPS:
            peer = along_x(k)
            to = device(z, peer, c)
            act(True, remote(ca.at[ch, peer], ga.at[ch, x], first_send.at[0], first_recv.at[ch, 0], to))
            act(True, remote(sa.at[ch, peer], gsa.at[ch, x], first_send.at[1], first_recv.at[ch, 1], to))
        for zi in range(2):
            zz = 2 * c + zi
            to = device(zz, x, c)
            act(zz != z, remote(cb.at[ch, zi], gb.at[ch, z], first_send.at[2], first_recv.at[ch, 2], to))
            act(zz != z, remote(sb.at[ch, zi], gsb.at[ch, z], first_send.at[3], first_recv.at[ch, 3], to))

    def act_start(condition, copy):
        if condition is True:
            copy.start()
        else:
            @pl.when(condition)
            def _():
                copy.start()

    def compute(ch):
        s = scores(ch, 0)
        for kv in range(KV_HALF):
            later = scores(ch, kv + 1) if kv + 1 < KV_HALF else None
            attend(ch, kv, s)
            s = later
        first_copies(ch, act_start)
        ga[ch, x] = ca[ch, x]
        gsa[ch, x] = sa[ch, x]

        @pl.when(merger)
        def _():
            zi = lax.rem(z, 2)
            gb[ch, z] = cb[ch, zi]
            gsb[ch, z] = sb[ch, zi]

    def weigh(parts):
        top = functools.reduce(jnp.maximum, parts)
        factors = [jnp.exp2(part - top) for part in parts]
        total = functools.reduce(jnp.add, factors)
        return [factor / total for factor in factors], top + jnp.log2(total)

    def merge_side(ch, count, got, stats, done):
        tiles = [stats[ch, i] for i in range(SIDE)]
        factors, logs = weigh([tile[:count] for tile in tiles])
        scales = [factors[i] * tiles[i][count : 2 * count] for i in range(SIDE)]
        for head in range(count):
            cols = slice(head * DH, (head + 1) * DH)
            added = functools.reduce(
                jnp.add,
                [
                    to_column(scales[i][head : head + 1]) * got[ch, i, :, cols].astype(jnp.int32).astype(jnp.float32)
                    for i in range(SIDE)
                ],
            )
            done[ch, head, 0:ROWS] = added
            done[ch, head, ROWS : ROWS + 8] = jnp.broadcast_to(logs[head : head + 1], (8, 128))

    def merge(ch):
        wait(ga.at[ch, 0 : SIDE - 1], first_recv.at[ch, 0])
        wait(gsa.at[ch, 0 : SIDE - 1], first_recv.at[ch, 1])
        merge_side(ch, 4, ga, gsa, da)
        for place in range(4):
            zz, core = 2 * c + place // 2, place % 2
            here = jnp.logical_and(zz == z, core == c)
            act_start(
                jnp.logical_not(here),
                remote(
                    da.at[ch, place], ha.at[ch, z], second_send.at[0], second_recv.at[ch, 0], device(zz, x, core)
                ),
            )

            @pl.when(here)
            def _():
                ha[ch, z] = da[ch, place]

        @pl.when(merger)
        def _():
            wait(gb.at[ch, 0 : SIDE - 1], first_recv.at[ch, 2])
            wait(gsb.at[ch, 0 : SIDE - 1], first_recv.at[ch, 3])
            merge_side(ch, 8, gb, gsb, db)
            for place in range(8):
                xx, core = place // 2, place % 2
                here = jnp.logical_and(xx == x, core == c)
                act_start(
                    jnp.logical_not(here),
                    remote(
                        db.at[ch, place], hb.at[ch, x], second_send.at[1], second_recv.at[ch, 1], device(z, xx, core)
                    ),
                )

                @pl.when(here)
                def _():
                    hb[ch, x] = db[ch, place]

    def finish(ch):
        for side, got in ((0, ha), (1, hb)):
            @pl.when(merger)
            def _():
                wait(got.at[ch, 0 : SIDE - 1], second_recv.at[ch, side])

            @pl.when(jnp.logical_not(merger))
            def _():
                wait(got.at[ch], second_recv.at[ch, side])

            factors, _ = weigh([got[ch, i, ROWS : ROWS + 1] for i in range(SIDE)])
            added = functools.reduce(jnp.add, [to_column(factors[i]) * got[ch, i, 0:ROWS] for i in range(SIDE)])
            out_ref[ch * ROWS : (ch + 1) * ROWS, side * DH : (side + 1) * DH] = added.astype(jnp.bfloat16)

    for ch in range(CHUNKS):
        spread_wait(ch, 2)
        compute(ch)
        if ch > 0:
            merge(ch - 1)
    merge(CHUNKS - 1)
    for ch in range(CHUNKS):
        finish(ch)

    wait(cand.at[:, 0], core_send)
    wait(lens.at[0], kv_send.at[0])
    wait(raw.at[0], kv_send.at[1])
    for stage in range(3):
        wait(r1.at[:, :, 0 : SIDE - 1], q_send.at[stage])
    wait(ga.at[:, 0 : SIDE - 1], first_send.at[0])
    wait(gsa.at[:, 0 : SIDE - 1], first_send.at[1])

    @pl.when(merger)
    def _():
        wait(gb.at[:, 0:1], first_send.at[2])
        wait(gsb.at[:, 0:1], first_send.at[3])
        wait(da.at[:, 0:3], second_send.at[0])
        wait(db.at[:, 0:7], second_send.at[1])

    @pl.when(jnp.logical_not(merger))
    def _():
        wait(gb.at[:, 0:2], first_send.at[2])
        wait(gsb.at[:, 0:2], first_send.at[3])
        wait(da, second_send.at[0])


def on_device(queries, keys, values, lengths, owner):
    vmem, dma = pltpu.VMEM, pltpu.SemaphoreType.DMA
    any_space = pl.BlockSpec(memory_space=pl.ANY)
    smem = pl.BlockSpec(memory_space=pltpu.SMEM)
    bf16, f32, i16 = jnp.bfloat16, jnp.float32, jnp.int16
    return pl.pallas_call(
        kernel,
        out_shape=jax.ShapeDtypeStruct((Q, 2 * DH), bf16),
        in_specs=[smem, smem, any_space, any_space, any_space],
        out_specs=pl.BlockSpec(memory_space=vmem),
        scratch_shapes=[
            vmem((CHUNKS, 2, ROWS, HALF), bf16),
            vmem((CHUNKS, ROWS, HALF), bf16),
            vmem((CHUNKS, 2, SIDE, ROWS, QUARTER), bf16),
            vmem((CHUNKS, 2, SIDE, ROWS, QUARTER), bf16),
            vmem((CHUNKS, ROWS, HALF), bf16),
            vmem((2, 2, BLK, KV_HALF * DH), bf16),
            vmem((2, 8, 128), jnp.int32),
            vmem((KV_HALF, 2 * DH, 2 * BLK), bf16),
            vmem((KV_HALF, 2 * BLK, 2 * DH), bf16),
            vmem((CHUNKS, SIDE, ROWS, 4 * DH), i16),
            vmem((CHUNKS, SIDE, 8, 128), f32),
            vmem((CHUNKS, 2, ROWS, 8 * DH), i16),
            vmem((CHUNKS, 2, 16, 128), f32),
            vmem((CHUNKS, SIDE, ROWS, 4 * DH), i16),
            vmem((CHUNKS, SIDE, 8, 128), f32),
            vmem((CHUNKS, SIDE, ROWS, 8 * DH), i16),
            vmem((CHUNKS, SIDE, 16, 128), f32),
            vmem((CHUNKS, 4, ROWS + 8, DH), f32),
            vmem((CHUNKS, 8, ROWS + 8, DH), f32),
            vmem((CHUNKS, SIDE, ROWS + 8, DH), f32),
            vmem((CHUNKS, SIDE, ROWS + 8, DH), f32),
            dma, dma((CHUNKS,)),
            dma((2,)), dma((2,)),
            dma((CHUNKS + 2,)),
            dma((3,)), dma((CHUNKS, 3)),
            dma((4,)), dma((CHUNKS, 4)),
            dma((2,)), dma((CHUNKS, 2)),
        ],
        compiler_params=pltpu.CompilerParams(
            collective_id=0, has_side_effects=True, vmem_limit_bytes=56 * 2**20
        ),
        cost_estimate=pl.CostEstimate(
            flops=4 * H * Q * BLK * DH, bytes_accessed=6 * 2**20, transcendentals=H * Q * BLK
        ),
    )(lengths, owner, queries, keys, values)


def solution(mesh):
    in_specs = (
        P(("req", "ctx"), None),
        P(("req", "ctx"), None),
        P(("req", "ctx"), None),
        P(("req", "ctx")),
        P("req"),
    )
    return jax.shard_map(
        on_device, mesh=mesh, in_specs=in_specs, out_specs=P("req", "ctx"), check_vma=False
    )
```

```python
import functools
import math

import jax
import jax.numpy as jnp
from jax import lax
from jax.experimental import pallas as pl
from jax.experimental.pallas import tpu as pltpu
from jax.sharding import PartitionSpec as P

H = 64
KVH = 8
DH = 128
Q = 128
BLK = 1024
GROUP = H // KVH
HALF = H * DH // 2
KV_HALF = KVH // 2
SIDE = 4
QUARTER = HALF // 2 // SIDE
SIZES = (32, 64, 32)
CHUNKS = len(SIZES)
STARTS = tuple(sum(SIZES[:ch]) for ch in range(CHUNKS))
SCALE = DH**-0.5 * math.log2(math.e)
STEPS = 32000.0
TINY = 1e-30
MESH = pl.DeviceIdType.MESH
HOPS = (2, 1, 3)
AB = (((1,), (0,)), ((), ()))


ORDER = (
    *[("offer", ch) for ch in range(CHUNKS)],
    ("keys",),
    ("prepare", 0),
    *[("across", ch) for ch in range(CHUNKS)],
    ("prepare", 1),
    *[("gather", ch) for ch in range(CHUNKS)],
    ("arrive", 0), ("compute", 0),
    ("arrive", 1), ("compute", 1), ("merge", 0),
    ("arrive", 2), ("compute", 2), ("merge", 1),
    ("finish", 0), ("merge", 2), ("finish", 1), ("finish", 2),
)


def rows_of(ch):
    return pl.ds(STARTS[ch], SIZES[ch])


def boxed(ch):
    return pl.ds(STARTS[ch] + 8 * ch, SIZES[ch] + 8)


def pick(index, parts):
    out = parts[-1]
    for i in range(len(parts) - 2, -1, -1):
        out = jnp.where(index == i, parts[i], out)
    return out


def kernel(
    lengths_ref, owner_ref, queries_ref, keys_ref, values_ref, out_ref,
    cand, s1, r1, r2, qf, raw, lens, kt, va,
    ca, sa, cb, sb, ga, gsa, gb, gsb, da, db, ha, hb,
    core_send, core_recv, kv_send, kv_recv, own_sem, q_send, q_recv,
    first_send, first_recv, second_send, second_recv,
):
    req = lax.axis_index("req")
    me = lax.axis_index("ctx")
    c = lax.rem(me, 2)
    x = lax.rem(me // 2, SIDE)
    z = me // (2 * SIDE)
    owner = owner_ref[0]
    owner_c = lax.rem(owner, 2)
    owner_x = lax.rem(owner // 2, SIDE)
    owner_z = owner // (2 * SIDE)

    def device(zz, xx, cc):
        return (req, (zz * SIDE + xx) * 2 + cc)

    def along_x(k):
        return lax.rem(x + k, SIDE)

    def along_z(k):
        return lax.rem(z + k, SIDE)

    sibling = device(z, x, 1 - c)

    def wait(ref, sem):
        pltpu.make_async_copy(ref, ref, sem).wait()

    def remote(src, dst, send, recv, to):
        return pltpu.make_async_remote_copy(
            src_ref=src, dst_ref=dst, send_sem=send, recv_sem=recv, device_id=to, device_id_type=MESH
        )

    barrier = pltpu.get_barrier_semaphore()
    peers = [sibling]
    for k in (1, 2, 3):
        for core in range(2):
            peers += [device(z, along_x(k), core), device(along_z(k), x, core)]
    for to in peers:
        pl.semaphore_signal(barrier, inc=1, device_id=to, device_id_type=MESH)

    own_cols = pl.ds(pl.multiple_of(c * HALF, HALF), HALF)
    sib_cols = pl.ds(pl.multiple_of((1 - c) * HALF, HALF), HALF)
    kv_width = KV_HALF * DH
    own_kv = pl.ds(pl.multiple_of(c * kv_width, kv_width), kv_width)
    sib_kv = pl.ds(pl.multiple_of((1 - c) * kv_width, kv_width), kv_width)

    own = [
        pltpu.make_async_copy(
            queries_ref.at[rows_of(ch), own_cols], cand.at[c, rows_of(ch)], own_sem.at[ch]
        )
        for ch in range(CHUNKS)
    ]
    own_k = pltpu.make_async_copy(keys_ref.at[:, own_kv], raw.at[c, 0], own_sem.at[CHUNKS])
    own_v = pltpu.make_async_copy(values_ref.at[:, own_kv], raw.at[c, 1], own_sem.at[CHUNKS + 1])
    for copy in own + [own_k, own_v]:
        copy.start()
    lens[c] = jnp.full((8, 128), lengths_ref[0], jnp.int32)

    pl.semaphore_wait(barrier, len(peers))

    core_q = [
        remote(
            queries_ref.at[rows_of(ch), sib_cols], cand.at[c, rows_of(ch)],
            core_send, core_recv.at[ch], sibling,
        )
        for ch in range(CHUNKS)
    ]
    core_kv = [
        remote(lens.at[c], lens.at[c], kv_send.at[0], kv_recv.at[0], sibling),
        remote(keys_ref.at[:, sib_kv], raw.at[c, 0], kv_send.at[1], kv_recv.at[1], sibling),
        remote(values_ref.at[:, sib_kv], raw.at[c, 1], kv_send.at[1], kv_recv.at[1], sibling),
    ]
    for copy in core_q + core_kv:
        copy.start()

    def quarter(index, half):
        return pl.ds(pl.multiple_of(half * (HALF // 2) + index * QUARTER, QUARTER), QUARTER)

    def spread_copies(ch, stage):
        copies = []
        for k in HOPS:
            for half in range(2):
                on_x = (stage + half) % 2 == 0
                to = device(z, along_x(k), c) if on_x else device(along_z(k), x, c)
                peer = along_x(k) if on_x else along_z(k)
                here = x if on_x else z
                if stage == 0:
                    src, dst = s1.at[rows_of(ch), quarter(peer, half)], r1.at[half, here, rows_of(ch)]
                elif stage == 1:
                    src = dst = r2.at[half, here, rows_of(ch)]
                else:
                    src = dst = qf.at[rows_of(ch), quarter(here, half)]
                copies.append(remote(src, dst, q_send.at[stage], q_recv.at[ch, stage], to))
        return copies

    def spread_wait(ch, stage):
        wait(r1.at[:, 0 : SIDE - 1, rows_of(ch)], q_recv.at[ch, stage])

    def offer(ch):
        own[ch].wait()
        core_q[ch].wait_recv()
        rows = rows_of(ch)
        s1[rows] = pick(owner_c, [cand[0, rows], cand[1, rows]])
        for copy in spread_copies(ch, 0):
            copy.start()
        r1[0, x, rows] = s1[rows, quarter(x, 0)]
        r1[1, z, rows] = s1[rows, quarter(z, 1)]

    def prepare(block):
        valid = lax.broadcasted_iota(jnp.int32, (BLK, DH), 0) < lens[block, 0:1, :]
        ones = jnp.where(valid, 1.0, 0.0).astype(jnp.bfloat16)
        rows = pl.ds(block * BLK, BLK)
        for kv in range(KV_HALF):
            cols = slice(kv * DH, (kv + 1) * DH)
            head = raw[block, 0, :, cols].astype(jnp.float32)
            head = jnp.where(valid, head, jnp.concatenate([head[:DH]] * (BLK // DH), axis=0)) * SCALE
            high = head.astype(jnp.bfloat16)
            low = (head - high.astype(jnp.float32)).astype(jnp.bfloat16)
            kt[kv, 0:DH, rows] = high.T
            kt[kv, DH : 2 * DH, rows] = low.T
            value = raw[block, 1, :, cols].astype(jnp.float32)
            va[kv, rows, 0:DH] = jnp.where(valid, value, 0.0).astype(jnp.bfloat16)
            va[kv, rows, DH : 2 * DH] = ones

    def keys_arrive():
        own_k.wait()
        own_v.wait()
        wait(lens.at[0], kv_recv.at[0])
        wait(raw.at[0], kv_recv.at[1])

    def across(ch):
        spread_wait(ch, 0)
        rows = rows_of(ch)
        r2[0, z, rows] = pick(owner_x, [r1[0, i, rows] for i in range(SIDE)])
        r2[1, x, rows] = pick(owner_z, [r1[1, i, rows] for i in range(SIDE)])
        for copy in spread_copies(ch, 1):
            copy.start()

    def gather(ch):
        spread_wait(ch, 1)
        rows = rows_of(ch)
        qf[rows, quarter(x, 0)] = pick(owner_z, [r2[0, i, rows] for i in range(SIDE)])
        qf[rows, quarter(z, 1)] = pick(owner_x, [r2[1, i, rows] for i in range(SIDE)])
        for copy in spread_copies(ch, 2):
            copy.start()

    def diagonal(size):
        return lax.broadcasted_iota(jnp.int32, (size, 128), 0) == lax.broadcasted_iota(jnp.int32, (size, 128), 1)

    def to_row(wide):
        return jnp.sum(jnp.where(diagonal(wide.shape[-2]), wide, 0.0), axis=-2)

    def to_column(row, size):
        return jnp.sum(jnp.where(diagonal(size), row, 0.0), axis=1, keepdims=True)

    def scores(ch, kv):
        rows = [qf[rows_of(ch), (kv * GROUP + i) * DH : (kv * GROUP + i + 1) * DH] for i in range(GROUP)]
        rows = jnp.concatenate(rows, axis=0)
        rows = jnp.concatenate([rows, rows], axis=1)
        return lax.dot_general(rows, kt[kv], AB, preferred_element_type=jnp.float32)

    def attend(ch, kv, s):
        tops, sums = [], []
        for block in range(2):
            part = s[:, block * BLK : (block + 1) * BLK]
            top = jnp.max(part, axis=1, keepdims=True)
            weights = jnp.exp2(part - top).astype(jnp.bfloat16)
            rows = slice(block * BLK, (block + 1) * BLK)
            sums.append(lax.dot_general(weights, va[kv, rows], AB, preferred_element_type=jnp.float32))
            tops.append(top)
        highest = jnp.maximum(tops[0], tops[1])
        both = jnp.exp2(tops[0] - highest) * sums[0] + jnp.exp2(tops[1] - highest) * sums[1]
        totals = both[:, DH:]
        largest = jnp.max(jnp.abs(both[:, :DH]), axis=1, keepdims=True)
        largest = jnp.maximum(largest, TINY)
        partial = jnp.round(both[:, :DH] * (STEPS / largest)).astype(jnp.int32).astype(jnp.int16)
        step = largest * (1.0 / STEPS) / totals
        log_total = highest + jnp.log2(totals)
        log_rows = to_row(log_total.reshape(GROUP, SIZES[ch], DH))
        step_rows = to_row(step.reshape(GROUP, SIZES[ch], DH))
        zi = kv // 2
        for i in range(GROUP):
            xx, core = (kv % 2) * 2 + i // 4, (i % 4) // 2
            part = partial[i * SIZES[ch] : (i + 1) * SIZES[ch]]
            if i % 2 == 0:
                place, to, box, stats, count = zi * 2 + core, xx, ca, sa, 4
            else:
                place, to, box, stats, count = xx * 2 + core, zi, cb, sb, 8
            box[to, rows_of(ch), place * DH : (place + 1) * DH] = part
            stats[ch, to, place : place + 1] = log_rows[i : i + 1]
            stats[ch, to, count + place : count + place + 1] = step_rows[i : i + 1]

    merger = c == z // 2

    def first_copies(ch, act):
        for k in HOPS:
            peer = along_x(k)
            to = device(z, peer, c)
            act(True, remote(ca.at[peer, rows_of(ch)], ga.at[x, rows_of(ch)], first_send.at[0], first_recv.at[ch, 0], to))
            act(True, remote(sa.at[ch, peer], gsa.at[ch, x], first_send.at[1], first_recv.at[ch, 1], to))
        for zi in range(2):
            zz = 2 * c + zi
            to = device(zz, x, c)
            act(zz != z, remote(cb.at[zi, rows_of(ch)], gb.at[z, rows_of(ch)], first_send.at[2], first_recv.at[ch, 2], to))
            act(zz != z, remote(sb.at[ch, zi], gsb.at[ch, z], first_send.at[3], first_recv.at[ch, 3], to))

    def act_start(condition, copy):
        if condition is True:
            copy.start()
        else:
            @pl.when(condition)
            def _():
                copy.start()

    def compute(ch):
        heads(ch, 0, KV_HALF)
        push(ch)

    def heads(ch, start, stop):
        s = scores(ch, start)
        for kv in range(start, stop):
            later = scores(ch, kv + 1) if kv + 1 < stop else None
            attend(ch, kv, s)
            s = later

    def push(ch):
        first_copies(ch, act_start)
        rows = rows_of(ch)
        ga[x, rows] = ca[x, rows]
        gsa[ch, x] = sa[ch, x]

        @pl.when(merger)
        def _():
            zi = lax.rem(z, 2)
            gb[z, rows] = cb[zi, rows]
            gsb[ch, z] = sb[ch, zi]

    def weigh(parts):
        top = functools.reduce(jnp.maximum, parts)
        factors = [jnp.exp2(part - top) for part in parts]
        total = functools.reduce(jnp.add, factors)
        return [factor / total for factor in factors], top + jnp.log2(total)

    def merge_side(ch, count, got, stats, done):
        tiles = [stats[ch, i] for i in range(SIDE)]
        factors, logs = weigh([tile[:count] for tile in tiles])
        scales = [factors[i] * tiles[i][count : 2 * count] for i in range(SIDE)]
        for head in range(count):
            cols = slice(head * DH, (head + 1) * DH)
            added = functools.reduce(
                jnp.add,
                [
                    to_column(scales[i][head : head + 1], SIZES[ch]) * got[i, rows_of(ch), cols].astype(jnp.int32).astype(jnp.float32)
                    for i in range(SIDE)
                ],
            )
            done[head, boxed(ch)] = jnp.concatenate([added, jnp.broadcast_to(logs[head : head + 1], (8, 128))], axis=0)

    def merge(ch):
        wait(ga.at[0 : SIDE - 1, rows_of(ch)], first_recv.at[ch, 0])
        wait(gsa.at[ch, 0 : SIDE - 1], first_recv.at[ch, 1])
        merge_side(ch, 4, ga, gsa, da)
        for place in range(4):
            zz, core = 2 * c + place // 2, place % 2
            here = jnp.logical_and(zz == z, core == c)
            act_start(
                jnp.logical_not(here),
                remote(
                    da.at[place, boxed(ch)], ha.at[z, boxed(ch)], second_send.at[0], second_recv.at[ch, 0], device(zz, x, core)
                ),
            )

            @pl.when(here)
            def _():
                ha[z, boxed(ch)] = da[place, boxed(ch)]

        @pl.when(merger)
        def _():
            wait(gb.at[0 : SIDE - 1, rows_of(ch)], first_recv.at[ch, 2])
            wait(gsb.at[ch, 0 : SIDE - 1], first_recv.at[ch, 3])
            merge_side(ch, 8, gb, gsb, db)
            for place in range(8):
                xx, core = place // 2, place % 2
                here = jnp.logical_and(xx == x, core == c)
                act_start(
                    jnp.logical_not(here),
                    remote(
                        db.at[place, boxed(ch)], hb.at[x, boxed(ch)], second_send.at[1], second_recv.at[ch, 1], device(z, xx, core)
                    ),
                )

                @pl.when(here)
                def _():
                    hb[x, boxed(ch)] = db[place, boxed(ch)]

    def finish(ch):
        for side, got in ((0, ha), (1, hb)):
            @pl.when(merger)
            def _():
                wait(got.at[0 : SIDE - 1, boxed(ch)], second_recv.at[ch, side])

            @pl.when(jnp.logical_not(merger))
            def _():
                wait(got.at[:, boxed(ch)], second_recv.at[ch, side])

            size, first = SIZES[ch], STARTS[ch] + 8 * ch
            factors, _ = weigh([got[i, first + size : first + size + 1] for i in range(SIDE)])
            added = functools.reduce(
                jnp.add, [to_column(factors[i], size) * got[i, first : first + size] for i in range(SIDE)]
            )
            out_ref[rows_of(ch), side * DH : (side + 1) * DH] = added.astype(jnp.bfloat16)

    steps = {
        "offer": offer, "keys": keys_arrive, "prepare": prepare, "across": across, "gather": gather,
        "arrive": lambda ch: spread_wait(ch, 2), "heads": heads, "push": push, "compute": compute,
        "merge": merge, "finish": finish,
    }
    for name, *at in ORDER:
        steps[name](*at)

    wait(cand.at[0], core_send)
    wait(lens.at[0], kv_send.at[0])
    wait(raw.at[0], kv_send.at[1])
    for stage in range(3):
        wait(r1.at[:, 0 : SIDE - 1], q_send.at[stage])
    wait(ga.at[0 : SIDE - 1], first_send.at[0])
    wait(gsa.at[:, 0 : SIDE - 1], first_send.at[1])

    @pl.when(merger)
    def _():
        wait(gb.at[0:1], first_send.at[2])
        wait(gsb.at[:, 0:1], first_send.at[3])
        wait(da.at[0:3], second_send.at[0])
        wait(db.at[0:7], second_send.at[1])

    @pl.when(jnp.logical_not(merger))
    def _():
        wait(gb.at[0:2], first_send.at[2])
        wait(gsb.at[:, 0:2], first_send.at[3])
        wait(da, second_send.at[0])


def on_device(queries, keys, values, lengths, owner):
    vmem, dma = pltpu.VMEM, pltpu.SemaphoreType.DMA
    any_space = pl.BlockSpec(memory_space=pl.ANY)
    smem = pl.BlockSpec(memory_space=pltpu.SMEM)
    bf16, f32, i16 = jnp.bfloat16, jnp.float32, jnp.int16
    return pl.pallas_call(
        kernel,
        out_shape=jax.ShapeDtypeStruct((Q, 2 * DH), bf16),
        in_specs=[smem, smem, any_space, any_space, any_space],
        out_specs=pl.BlockSpec(memory_space=vmem),
        scratch_shapes=[
            vmem((2, Q, HALF), bf16),
            vmem((Q, HALF), bf16),
            vmem((2, SIDE, Q, QUARTER), bf16),
            vmem((2, SIDE, Q, QUARTER), bf16),
            vmem((Q, HALF), bf16),
            vmem((2, 2, BLK, KV_HALF * DH), bf16),
            vmem((2, 8, 128), jnp.int32),
            vmem((KV_HALF, 2 * DH, 2 * BLK), bf16),
            vmem((KV_HALF, 2 * BLK, 2 * DH), bf16),
            vmem((SIDE, Q, 4 * DH), i16),
            vmem((CHUNKS, SIDE, 8, 128), f32),
            vmem((2, Q, 8 * DH), i16),
            vmem((CHUNKS, 2, 16, 128), f32),
            vmem((SIDE, Q, 4 * DH), i16),
            vmem((CHUNKS, SIDE, 8, 128), f32),
            vmem((SIDE, Q, 8 * DH), i16),
            vmem((CHUNKS, SIDE, 16, 128), f32),
            vmem((4, Q + 8 * CHUNKS, DH), f32),
            vmem((8, Q + 8 * CHUNKS, DH), f32),
            vmem((SIDE, Q + 8 * CHUNKS, DH), f32),
            vmem((SIDE, Q + 8 * CHUNKS, DH), f32),
            dma, dma((CHUNKS,)),
            dma((2,)), dma((2,)),
            dma((CHUNKS + 2,)),
            dma((3,)), dma((CHUNKS, 3)),
            dma((4,)), dma((CHUNKS, 4)),
            dma((2,)), dma((CHUNKS, 2)),
        ],
        compiler_params=pltpu.CompilerParams(
            collective_id=0, has_side_effects=True, vmem_limit_bytes=56 * 2**20
        ),
        cost_estimate=pl.CostEstimate(
            flops=4 * H * Q * BLK * DH, bytes_accessed=6 * 2**20, transcendentals=H * Q * BLK
        ),
    )(lengths, owner, queries, keys, values)


def solution(mesh):
    in_specs = (
        P(("req", "ctx"), None),
        P(("req", "ctx"), None),
        P(("req", "ctx"), None),
        P(("req", "ctx")),
        P("req"),
    )
    return jax.shard_map(
        on_device, mesh=mesh, in_specs=in_specs, out_specs=P("req", "ctx"), check_vma=False
    )
```

```python
import functools
import math

import jax
import jax.numpy as jnp
from jax import lax
from jax.experimental import pallas as pl
from jax.experimental.pallas import tpu as pltpu
from jax.sharding import PartitionSpec as P

H = 64
KVH = 8
DH = 128
Q = 128
BLK = 1024
GROUP = H // KVH
HALF = H * DH // 2
KV_HALF = KVH // 2
SIDE = 4
QUARTER = HALF // 2 // SIDE
SIZES = (32, 64, 32)
CHUNKS = len(SIZES)
STARTS = tuple(sum(SIZES[:ch]) for ch in range(CHUNKS))
SCALE = DH**-0.5 * math.log2(math.e)
STEPS = 32000.0
TINY = 1e-30
MESH = pl.DeviceIdType.MESH
HOPS = (2, 1, 3)
AB = (((1,), (0,)), ((), ()))


EARLY = (1,)
ORDER = (
    *[("offer", ch) for ch in range(CHUNKS)],
    ("keys",),
    ("prepare", 0),
    *[("across", ch) for ch in range(CHUNKS)],
    ("prepare", 1),
    *[("gather", ch) for ch in range(CHUNKS)],
    ("arrive", 0), ("compute", 0),
    ("arrive", 1), ("compute", 1), ("merge", 0),
    ("arrive", 2), ("compute", 2), ("merge", 1),
    ("finish", 0), ("merge", 2), ("finish", 1), ("finish", 2),
)


def rows_of(ch):
    return pl.ds(STARTS[ch], SIZES[ch])


def boxed(ch):
    return pl.ds(STARTS[ch] + 8 * ch, SIZES[ch] + 8)


def pick(index, parts):
    out = parts[-1]
    for i in range(len(parts) - 2, -1, -1):
        out = jnp.where(index == i, parts[i], out)
    return out


def kernel(
    lengths_ref, owner_ref, queries_ref, keys_ref, values_ref, out_ref,
    cand, s1, r1, r2, qf, raw, lens, kt, va,
    ca, sa, cb, sb, ga, gsa, gb, gsb, da, db, ha, hb,
    core_send, core_recv, kv_send, kv_recv, own_sem, q_send, q_recv,
    first_send, first_recv, second_send, second_recv,
):
    req = lax.axis_index("req")
    me = lax.axis_index("ctx")
    c = lax.rem(me, 2)
    x = lax.rem(me // 2, SIDE)
    z = me // (2 * SIDE)
    owner = owner_ref[0]
    owner_c = lax.rem(owner, 2)
    owner_x = lax.rem(owner // 2, SIDE)
    owner_z = owner // (2 * SIDE)

    def device(zz, xx, cc):
        return (req, (zz * SIDE + xx) * 2 + cc)

    def along_x(k):
        return lax.rem(x + k, SIDE)

    def along_z(k):
        return lax.rem(z + k, SIDE)

    sibling = device(z, x, 1 - c)

    def wait(ref, sem):
        pltpu.make_async_copy(ref, ref, sem).wait()

    def remote(src, dst, send, recv, to):
        return pltpu.make_async_remote_copy(
            src_ref=src, dst_ref=dst, send_sem=send, recv_sem=recv, device_id=to, device_id_type=MESH
        )

    barrier = pltpu.get_barrier_semaphore()
    peers = []
    for k in HOPS:
        for core in range(2):
            peers += [device(z, along_x(k), core), device(along_z(k), x, core)]
    peers.append(sibling)
    for to in peers:
        pl.semaphore_signal(barrier, inc=1, device_id=to, device_id_type=MESH)

    own_cols = pl.ds(pl.multiple_of(c * HALF, HALF), HALF)
    sib_cols = pl.ds(pl.multiple_of((1 - c) * HALF, HALF), HALF)
    kv_width = KV_HALF * DH
    own_kv = pl.ds(pl.multiple_of(c * kv_width, kv_width), kv_width)
    sib_kv = pl.ds(pl.multiple_of((1 - c) * kv_width, kv_width), kv_width)

    own = [
        pltpu.make_async_copy(
            queries_ref.at[rows_of(ch), own_cols], cand.at[c, rows_of(ch)], own_sem.at[ch]
        )
        for ch in range(CHUNKS)
    ]
    own_k = pltpu.make_async_copy(keys_ref.at[:, own_kv], raw.at[c, 0], own_sem.at[CHUNKS])
    own_v = pltpu.make_async_copy(values_ref.at[:, own_kv], raw.at[c, 1], own_sem.at[CHUNKS + 1])
    for copy in own + [own_k, own_v]:
        copy.start()
    lens[c] = jnp.full((8, 128), lengths_ref[0], jnp.int32)

    pl.semaphore_wait(barrier, len(peers))

    core_q = [
        remote(
            queries_ref.at[rows_of(ch), sib_cols], cand.at[c, rows_of(ch)],
            core_send, core_recv.at[ch], sibling,
        )
        for ch in range(CHUNKS)
    ]
    core_kv = [
        remote(lens.at[c], lens.at[c], kv_send.at[0], kv_recv.at[0], sibling),
        remote(keys_ref.at[:, sib_kv], raw.at[c, 0], kv_send.at[1], kv_recv.at[1], sibling),
        remote(values_ref.at[:, sib_kv], raw.at[c, 1], kv_send.at[1], kv_recv.at[1], sibling),
    ]
    for copy in core_q + core_kv:
        copy.start()

    def quarter(index, half):
        return pl.ds(pl.multiple_of(half * (HALF // 2) + index * QUARTER, QUARTER), QUARTER)

    def spread_copies(ch, stage):
        copies = []
        for k in HOPS:
            for half in range(2):
                on_x = (stage + half) % 2 == 0
                to = device(z, along_x(k), c) if on_x else device(along_z(k), x, c)
                peer = along_x(k) if on_x else along_z(k)
                here = x if on_x else z
                if stage == 0:
                    src, dst = s1.at[rows_of(ch), quarter(peer, half)], r1.at[half, here, rows_of(ch)]
                elif stage == 1:
                    src = dst = r2.at[half, here, rows_of(ch)]
                else:
                    src = dst = qf.at[rows_of(ch), quarter(here, half)]
                copies.append(remote(src, dst, q_send.at[stage], q_recv.at[ch, stage], to))
        return copies

    def spread_wait(ch, stage):
        wait(r1.at[:, 0 : SIDE - 1, rows_of(ch)], q_recv.at[ch, stage])

    def offer(ch):
        own[ch].wait()
        core_q[ch].wait_recv()
        rows = rows_of(ch)
        s1[rows] = pick(owner_c, [cand[0, rows], cand[1, rows]])
        for copy in spread_copies(ch, 0):
            copy.start()
        r1[0, x, rows] = s1[rows, quarter(x, 0)]
        r1[1, z, rows] = s1[rows, quarter(z, 1)]

    def prepare(block):
        valid = lax.broadcasted_iota(jnp.int32, (BLK, DH), 0) < lens[block, 0:1, :]
        ones = jnp.where(valid, 1.0, 0.0).astype(jnp.bfloat16)
        rows = pl.ds(block * BLK, BLK)
        for kv in range(KV_HALF):
            cols = slice(kv * DH, (kv + 1) * DH)
            head = raw[block, 0, :, cols].astype(jnp.float32)
            head = jnp.where(valid, head, jnp.concatenate([head[:DH]] * (BLK // DH), axis=0)) * SCALE
            high = head.astype(jnp.bfloat16)
            low = (head - high.astype(jnp.float32)).astype(jnp.bfloat16)
            kt[kv, 0:DH, rows] = high.T
            kt[kv, DH : 2 * DH, rows] = low.T
            value = raw[block, 1, :, cols].astype(jnp.float32)
            va[kv, rows, 0:DH] = jnp.where(valid, value, 0.0).astype(jnp.bfloat16)
            va[kv, rows, DH : 2 * DH] = ones

    def keys_arrive():
        own_k.wait()
        own_v.wait()
        wait(lens.at[0], kv_recv.at[0])
        wait(raw.at[0], kv_recv.at[1])

    def across(ch):
        spread_wait(ch, 0)
        rows = rows_of(ch)
        r2[0, z, rows] = pick(owner_x, [r1[0, i, rows] for i in range(SIDE)])
        r2[1, x, rows] = pick(owner_z, [r1[1, i, rows] for i in range(SIDE)])
        for copy in spread_copies(ch, 1):
            copy.start()

    def gather(ch):
        spread_wait(ch, 1)
        rows = rows_of(ch)
        qf[rows, quarter(x, 0)] = pick(owner_z, [r2[0, i, rows] for i in range(SIDE)])
        qf[rows, quarter(z, 1)] = pick(owner_x, [r2[1, i, rows] for i in range(SIDE)])
        for copy in spread_copies(ch, 2):
            copy.start()

    def diagonal(size):
        return lax.broadcasted_iota(jnp.int32, (size, 128), 0) == lax.broadcasted_iota(jnp.int32, (size, 128), 1)

    def to_row(wide):
        return jnp.sum(jnp.where(diagonal(wide.shape[-2]), wide, 0.0), axis=-2)

    def to_column(row, size):
        return jnp.sum(jnp.where(diagonal(size), row, 0.0), axis=1, keepdims=True)

    def scores(ch, kv):
        rows = [qf[rows_of(ch), (kv * GROUP + i) * DH : (kv * GROUP + i + 1) * DH] for i in range(GROUP)]
        rows = jnp.concatenate(rows, axis=0)
        rows = jnp.concatenate([rows, rows], axis=1)
        return lax.dot_general(rows, kt[kv], AB, preferred_element_type=jnp.float32)

    def attend(ch, kv, s):
        tops, sums = [], []
        for block in range(2):
            part = s[:, block * BLK : (block + 1) * BLK]
            top = jnp.max(part, axis=1, keepdims=True)
            weights = jnp.exp2(part - top).astype(jnp.bfloat16)
            rows = slice(block * BLK, (block + 1) * BLK)
            sums.append(lax.dot_general(weights, va[kv, rows], AB, preferred_element_type=jnp.float32))
            tops.append(top)
        highest = jnp.maximum(tops[0], tops[1])
        both = jnp.exp2(tops[0] - highest) * sums[0] + jnp.exp2(tops[1] - highest) * sums[1]
        totals = both[:, DH:]
        largest = jnp.max(jnp.abs(both[:, :DH]), axis=1, keepdims=True)
        largest = jnp.maximum(largest, TINY)
        partial = jnp.round(both[:, :DH] * (STEPS / largest)).astype(jnp.int32).astype(jnp.int16)
        step = largest * (1.0 / STEPS) / totals
        log_total = highest + jnp.log2(totals)
        log_rows = to_row(log_total.reshape(GROUP, SIZES[ch], DH))
        step_rows = to_row(step.reshape(GROUP, SIZES[ch], DH))
        zi = kv // 2
        for i in range(GROUP):
            xx, core = (kv % 2) * 2 + i // 4, (i % 4) // 2
            part = partial[i * SIZES[ch] : (i + 1) * SIZES[ch]]
            if i % 2 == 0:
                place, to, box, stats, count = zi * 2 + core, xx, ca, sa, 4
            else:
                place, to, box, stats, count = xx * 2 + core, zi, cb, sb, 8
            box[to, rows_of(ch), place * DH : (place + 1) * DH] = part
            stats[ch, to, place : place + 1] = log_rows[i : i + 1]
            stats[ch, to, count + place : count + place + 1] = step_rows[i : i + 1]

    merger = c == z // 2

    def act_start(condition, copy):
        if condition is True:
            copy.start()
        else:
            @pl.when(condition)
            def _():
                copy.start()

    def send_or_keep(here, pairs):
        for src, dst, send, recv, to in pairs:
            act_start(jnp.logical_not(here), remote(src, dst, send, recv, to))

        @pl.when(here)
        def _():
            for src, dst, *_ in pairs:
                dst[...] = src[...]

    def push_x(ch, xx):
        to, rows = device(z, xx, c), rows_of(ch)
        send_or_keep(
            xx == x,
            [
                (ca.at[xx, rows], ga.at[x, rows], first_send.at[0], first_recv.at[ch, 0], to),
                (sa.at[ch, xx], gsa.at[ch, x], first_send.at[1], first_recv.at[ch, 1], to),
            ],
        )

    def push_z(ch, zi):
        to, rows = device(2 * c + zi, x, c), rows_of(ch)
        send_or_keep(
            2 * c + zi == z,
            [
                (cb.at[zi, rows], gb.at[z, rows], first_send.at[2], first_recv.at[ch, 2], to),
                (sb.at[ch, zi], gsb.at[ch, z], first_send.at[3], first_recv.at[ch, 3], to),
            ],
        )

    def compute(ch):
        s = scores(ch, 0)
        for kv in range(KV_HALF):
            later = scores(ch, kv + 1) if kv + 1 < KV_HALF else None
            attend(ch, kv, s)
            s = later
            if kv in EARLY:
                push(ch, kv)
        for kv in range(KV_HALF):
            if kv not in EARLY:
                push(ch, kv)

    def push(ch, kv):
        if kv == 1:
            push_z(ch, 0)
        if kv == 2:
            push_x(ch, 0)
            push_x(ch, 1)
        if kv == 3:
            push_x(ch, 2)
            push_x(ch, 3)
            push_z(ch, 1)

    def weigh(parts):
        top = functools.reduce(jnp.maximum, parts)
        factors = [jnp.exp2(part - top) for part in parts]
        total = functools.reduce(jnp.add, factors)
        return [factor / total for factor in factors], top + jnp.log2(total)

    def merge_side(ch, count, got, stats, done):
        tiles = [stats[ch, i] for i in range(SIDE)]
        factors, logs = weigh([tile[:count] for tile in tiles])
        scales = [factors[i] * tiles[i][count : 2 * count] for i in range(SIDE)]
        for head in range(count):
            cols = slice(head * DH, (head + 1) * DH)
            added = functools.reduce(
                jnp.add,
                [
                    to_column(scales[i][head : head + 1], SIZES[ch]) * got[i, rows_of(ch), cols].astype(jnp.int32).astype(jnp.float32)
                    for i in range(SIDE)
                ],
            )
            done[head, boxed(ch)] = jnp.concatenate([added, jnp.broadcast_to(logs[head : head + 1], (8, 128))], axis=0)

    def merge(ch):
        wait(ga.at[0 : SIDE - 1, rows_of(ch)], first_recv.at[ch, 0])
        wait(gsa.at[ch, 0 : SIDE - 1], first_recv.at[ch, 1])
        merge_side(ch, 4, ga, gsa, da)
        for place in range(4):
            zz, core = 2 * c + place // 2, place % 2
            here = jnp.logical_and(zz == z, core == c)
            act_start(
                jnp.logical_not(here),
                remote(
                    da.at[place, boxed(ch)], ha.at[z, boxed(ch)], second_send.at[0], second_recv.at[ch, 0], device(zz, x, core)
                ),
            )

            @pl.when(here)
            def _():
                ha[z, boxed(ch)] = da[place, boxed(ch)]

        @pl.when(merger)
        def _():
            wait(gb.at[0 : SIDE - 1, rows_of(ch)], first_recv.at[ch, 2])
            wait(gsb.at[ch, 0 : SIDE - 1], first_recv.at[ch, 3])
            merge_side(ch, 8, gb, gsb, db)
            for place in range(8):
                xx, core = place // 2, place % 2
                here = jnp.logical_and(xx == x, core == c)
                act_start(
                    jnp.logical_not(here),
                    remote(
                        db.at[place, boxed(ch)], hb.at[x, boxed(ch)], second_send.at[1], second_recv.at[ch, 1], device(z, xx, core)
                    ),
                )

                @pl.when(here)
                def _():
                    hb[x, boxed(ch)] = db[place, boxed(ch)]

    def finish(ch):
        for side, got in ((0, ha), (1, hb)):
            @pl.when(merger)
            def _():
                wait(got.at[0 : SIDE - 1, boxed(ch)], second_recv.at[ch, side])

            @pl.when(jnp.logical_not(merger))
            def _():
                wait(got.at[:, boxed(ch)], second_recv.at[ch, side])

            size, first = SIZES[ch], STARTS[ch] + 8 * ch
            factors, _ = weigh([got[i, first + size : first + size + 1] for i in range(SIDE)])
            added = functools.reduce(
                jnp.add, [to_column(factors[i], size) * got[i, first : first + size] for i in range(SIDE)]
            )
            out_ref[rows_of(ch), side * DH : (side + 1) * DH] = added.astype(jnp.bfloat16)

    steps = {
        "offer": offer, "keys": keys_arrive, "prepare": prepare, "across": across, "gather": gather,
        "arrive": lambda ch: spread_wait(ch, 2), "compute": compute,
        "merge": merge, "finish": finish,
    }
    for name, *at in ORDER:
        steps[name](*at)

    wait(cand.at[0], core_send)
    wait(lens.at[0], kv_send.at[0])
    wait(raw.at[0], kv_send.at[1])
    for stage in range(3):
        wait(r1.at[:, 0 : SIDE - 1], q_send.at[stage])
    wait(ga.at[0 : SIDE - 1], first_send.at[0])
    wait(gsa.at[:, 0 : SIDE - 1], first_send.at[1])

    @pl.when(merger)
    def _():
        wait(gb.at[0:1], first_send.at[2])
        wait(gsb.at[:, 0:1], first_send.at[3])
        wait(da.at[0:3], second_send.at[0])
        wait(db.at[0:7], second_send.at[1])

    @pl.when(jnp.logical_not(merger))
    def _():
        wait(gb.at[0:2], first_send.at[2])
        wait(gsb.at[:, 0:2], first_send.at[3])
        wait(da, second_send.at[0])


def on_device(queries, keys, values, lengths, owner):
    vmem, dma = pltpu.VMEM, pltpu.SemaphoreType.DMA
    any_space = pl.BlockSpec(memory_space=pl.ANY)
    smem = pl.BlockSpec(memory_space=pltpu.SMEM)
    bf16, f32, i16 = jnp.bfloat16, jnp.float32, jnp.int16
    return pl.pallas_call(
        kernel,
        out_shape=jax.ShapeDtypeStruct((Q, 2 * DH), bf16),
        in_specs=[smem, smem, any_space, any_space, any_space],
        out_specs=pl.BlockSpec(memory_space=vmem),
        scratch_shapes=[
            vmem((2, Q, HALF), bf16),
            vmem((Q, HALF), bf16),
            vmem((2, SIDE, Q, QUARTER), bf16),
            vmem((2, SIDE, Q, QUARTER), bf16),
            vmem((Q, HALF), bf16),
            vmem((2, 2, BLK, KV_HALF * DH), bf16),
            vmem((2, 8, 128), jnp.int32),
            vmem((KV_HALF, 2 * DH, 2 * BLK), bf16),
            vmem((KV_HALF, 2 * BLK, 2 * DH), bf16),
            vmem((SIDE, Q, 4 * DH), i16),
            vmem((CHUNKS, SIDE, 8, 128), f32),
            vmem((2, Q, 8 * DH), i16),
            vmem((CHUNKS, 2, 16, 128), f32),
            vmem((SIDE, Q, 4 * DH), i16),
            vmem((CHUNKS, SIDE, 8, 128), f32),
            vmem((SIDE, Q, 8 * DH), i16),
            vmem((CHUNKS, SIDE, 16, 128), f32),
            vmem((4, Q + 8 * CHUNKS, DH), f32),
            vmem((8, Q + 8 * CHUNKS, DH), f32),
            vmem((SIDE, Q + 8 * CHUNKS, DH), f32),
            vmem((SIDE, Q + 8 * CHUNKS, DH), f32),
            dma, dma((CHUNKS,)),
            dma((2,)), dma((2,)),
            dma((CHUNKS + 2,)),
            dma((3,)), dma((CHUNKS, 3)),
            dma((4,)), dma((CHUNKS, 4)),
            dma((2,)), dma((CHUNKS, 2)),
        ],
        compiler_params=pltpu.CompilerParams(
            collective_id=0, has_side_effects=True, vmem_limit_bytes=56 * 2**20
        ),
        cost_estimate=pl.CostEstimate(
            flops=4 * H * Q * BLK * DH, bytes_accessed=6 * 2**20, transcendentals=H * Q * BLK
        ),
    )(lengths, owner, queries, keys, values)


def solution(mesh):
    in_specs = (
        P(("req", "ctx"), None),
        P(("req", "ctx"), None),
        P(("req", "ctx"), None),
        P(("req", "ctx")),
        P("req"),
    )
    return jax.shard_map(
        on_device, mesh=mesh, in_specs=in_specs, out_specs=P("req", "ctx"), check_vma=False
    )
```

```python
import functools
import math

import jax
import jax.numpy as jnp
from jax import lax
from jax.experimental import pallas as pl
from jax.experimental.pallas import tpu as pltpu
from jax.sharding import PartitionSpec as P

H = 64
KVH = 8
DH = 128
Q = 128
BLK = 1024
GROUP = H // KVH
HALF = H * DH // 2
KV_HALF = KVH // 2
SIDE = 4
QUARTER = HALF // 2 // SIDE
SIZES = (32, 64, 32)
CHUNKS = len(SIZES)
STARTS = tuple(sum(SIZES[:ch]) for ch in range(CHUNKS))
SCALE = DH**-0.5 * math.log2(math.e)
STEPS = 32000.0
TINY = 1e-30
MESH = pl.DeviceIdType.MESH
HOPS = (2, 1, 3)
AB = (((1,), (0,)), ((), ()))


EARLY = ((), (), (1, 2))
ORDER = (
    *[("offer", ch) for ch in range(CHUNKS)],
    ("keys",),
    ("prepare", 0),
    *[("across", ch) for ch in range(CHUNKS)],
    ("prepare", 1),
    *[("gather", ch) for ch in range(CHUNKS)],
    ("arrive", 0), ("compute", 0),
    ("arrive", 1), ("compute", 1), ("merge", 0),
    ("arrive", 2), ("compute", 2), ("merge", 1),
    ("finish", 0), ("merge", 2), ("finish", 1), ("finish", 2),
)


def rows_of(ch):
    return pl.ds(STARTS[ch], SIZES[ch])


def boxed(ch):
    return pl.ds(STARTS[ch] + 8 * ch, SIZES[ch] + 8)


def pick(index, parts):
    out = parts[-1]
    for i in range(len(parts) - 2, -1, -1):
        out = jnp.where(index == i, parts[i], out)
    return out


def kernel(
    lengths_ref, owner_ref, queries_ref, keys_ref, values_ref, out_ref,
    cand, s1, r1, r2, qf, raw, lens, kt, va,
    ca, sa, cb, sb, ga, gsa, gb, gsb, da, db, ha, hb,
    core_send, core_recv, kv_send, kv_recv, own_sem, q_send, q_recv,
    first_send, first_recv, second_send, second_recv,
):
    req = lax.axis_index("req")
    me = lax.axis_index("ctx")
    c = lax.rem(me, 2)
    x = lax.rem(me // 2, SIDE)
    z = me // (2 * SIDE)
    owner = owner_ref[0]
    owner_c = lax.rem(owner, 2)
    owner_x = lax.rem(owner // 2, SIDE)
    owner_z = owner // (2 * SIDE)

    def device(zz, xx, cc):
        return (req, (zz * SIDE + xx) * 2 + cc)

    def along_x(k):
        return lax.rem(x + k, SIDE)

    def along_z(k):
        return lax.rem(z + k, SIDE)

    sibling = device(z, x, 1 - c)

    def wait(ref, sem):
        pltpu.make_async_copy(ref, ref, sem).wait()

    def remote(src, dst, send, recv, to):
        return pltpu.make_async_remote_copy(
            src_ref=src, dst_ref=dst, send_sem=send, recv_sem=recv, device_id=to, device_id_type=MESH
        )

    barrier = pltpu.get_barrier_semaphore()
    peers = []
    for k in HOPS:
        for core in range(2):
            peers += [device(z, along_x(k), core), device(along_z(k), x, core)]
    peers.append(sibling)
    for to in peers:
        pl.semaphore_signal(barrier, inc=1, device_id=to, device_id_type=MESH)

    own_cols = pl.ds(pl.multiple_of(c * HALF, HALF), HALF)
    sib_cols = pl.ds(pl.multiple_of((1 - c) * HALF, HALF), HALF)
    kv_width = KV_HALF * DH
    own_kv = pl.ds(pl.multiple_of(c * kv_width, kv_width), kv_width)
    sib_kv = pl.ds(pl.multiple_of((1 - c) * kv_width, kv_width), kv_width)

    own = [
        pltpu.make_async_copy(
            queries_ref.at[rows_of(ch), own_cols], cand.at[c, rows_of(ch)], own_sem.at[ch]
        )
        for ch in range(CHUNKS)
    ]
    own_k = pltpu.make_async_copy(keys_ref.at[:, own_kv], raw.at[c, 0], own_sem.at[CHUNKS])
    own_v = pltpu.make_async_copy(values_ref.at[:, own_kv], raw.at[c, 1], own_sem.at[CHUNKS + 1])
    for copy in own + [own_k, own_v]:
        copy.start()
    lens[c] = jnp.full((8, 128), lengths_ref[0], jnp.int32)

    pl.semaphore_wait(barrier, len(peers))

    core_q = [
        remote(
            queries_ref.at[rows_of(ch), sib_cols], cand.at[c, rows_of(ch)],
            core_send, core_recv.at[ch], sibling,
        )
        for ch in range(CHUNKS)
    ]
    core_kv = [
        remote(lens.at[c], lens.at[c], kv_send.at[0], kv_recv.at[0], sibling),
        remote(keys_ref.at[:, sib_kv], raw.at[c, 0], kv_send.at[1], kv_recv.at[1], sibling),
        remote(values_ref.at[:, sib_kv], raw.at[c, 1], kv_send.at[1], kv_recv.at[1], sibling),
    ]
    for copy in core_q + core_kv:
        copy.start()

    def quarter(index, half):
        return pl.ds(pl.multiple_of(half * (HALF // 2) + index * QUARTER, QUARTER), QUARTER)

    def spread_copies(ch, stage):
        copies = []
        for k in HOPS:
            for half in range(2):
                on_x = (stage + half) % 2 == 0
                to = device(z, along_x(k), c) if on_x else device(along_z(k), x, c)
                peer = along_x(k) if on_x else along_z(k)
                here = x if on_x else z
                if stage == 0:
                    src, dst = s1.at[rows_of(ch), quarter(peer, half)], r1.at[half, here, rows_of(ch)]
                elif stage == 1:
                    src = dst = r2.at[half, here, rows_of(ch)]
                else:
                    src = dst = qf.at[rows_of(ch), quarter(here, half)]
                copies.append(remote(src, dst, q_send.at[stage], q_recv.at[ch, stage], to))
        return copies

    def spread_wait(ch, stage):
        wait(r1.at[:, 0 : SIDE - 1, rows_of(ch)], q_recv.at[ch, stage])

    def offer(ch):
        own[ch].wait()
        core_q[ch].wait_recv()
        rows = rows_of(ch)
        s1[rows] = pick(owner_c, [cand[0, rows], cand[1, rows]])
        for copy in spread_copies(ch, 0):
            copy.start()
        r1[0, x, rows] = s1[rows, quarter(x, 0)]
        r1[1, z, rows] = s1[rows, quarter(z, 1)]

    def prepare(block):
        valid = lax.broadcasted_iota(jnp.int32, (BLK, DH), 0) < lens[block, 0:1, :]
        ones = jnp.where(valid, 1.0, 0.0).astype(jnp.bfloat16)
        rows = pl.ds(block * BLK, BLK)
        for kv in range(KV_HALF):
            cols = slice(kv * DH, (kv + 1) * DH)
            head = raw[block, 0, :, cols].astype(jnp.float32)
            head = jnp.where(valid, head, jnp.concatenate([head[:DH]] * (BLK // DH), axis=0)) * SCALE
            high = head.astype(jnp.bfloat16)
            low = (head - high.astype(jnp.float32)).astype(jnp.bfloat16)
            kt[kv, 0:DH, rows] = high.T
            kt[kv, DH : 2 * DH, rows] = low.T
            value = raw[block, 1, :, cols].astype(jnp.float32)
            va[kv, rows, 0:DH] = jnp.where(valid, value, 0.0).astype(jnp.bfloat16)
            va[kv, rows, DH : 2 * DH] = ones

    def keys_arrive():
        own_k.wait()
        own_v.wait()
        wait(lens.at[0], kv_recv.at[0])
        wait(raw.at[0], kv_recv.at[1])

    def across(ch):
        spread_wait(ch, 0)
        rows = rows_of(ch)
        r2[0, z, rows] = pick(owner_x, [r1[0, i, rows] for i in range(SIDE)])
        r2[1, x, rows] = pick(owner_z, [r1[1, i, rows] for i in range(SIDE)])
        for copy in spread_copies(ch, 1):
            copy.start()

    def gather(ch):
        spread_wait(ch, 1)
        rows = rows_of(ch)
        qf[rows, quarter(x, 0)] = pick(owner_z, [r2[0, i, rows] for i in range(SIDE)])
        qf[rows, quarter(z, 1)] = pick(owner_x, [r2[1, i, rows] for i in range(SIDE)])
        for copy in spread_copies(ch, 2):
            copy.start()

    def diagonal(size):
        return lax.broadcasted_iota(jnp.int32, (size, 128), 0) == lax.broadcasted_iota(jnp.int32, (size, 128), 1)

    def to_row(wide):
        return jnp.sum(jnp.where(diagonal(wide.shape[-2]), wide, 0.0), axis=-2)

    def to_column(row, size):
        return jnp.sum(jnp.where(diagonal(size), row, 0.0), axis=1, keepdims=True)

    def scores(ch, kv):
        rows = [qf[rows_of(ch), (kv * GROUP + i) * DH : (kv * GROUP + i + 1) * DH] for i in range(GROUP)]
        rows = jnp.concatenate(rows, axis=0)
        rows = jnp.concatenate([rows, rows], axis=1)
        return lax.dot_general(rows, kt[kv], AB, preferred_element_type=jnp.float32)

    def attend(ch, kv, s):
        tops, sums = [], []
        for block in range(2):
            part = s[:, block * BLK : (block + 1) * BLK]
            top = jnp.max(part, axis=1, keepdims=True)
            weights = jnp.exp2(part - top).astype(jnp.bfloat16)
            rows = slice(block * BLK, (block + 1) * BLK)
            sums.append(lax.dot_general(weights, va[kv, rows], AB, preferred_element_type=jnp.float32))
            tops.append(top)
        highest = jnp.maximum(tops[0], tops[1])
        both = jnp.exp2(tops[0] - highest) * sums[0] + jnp.exp2(tops[1] - highest) * sums[1]
        totals = both[:, DH:]
        largest = jnp.max(jnp.abs(both[:, :DH]), axis=1, keepdims=True)
        largest = jnp.maximum(largest, TINY)
        partial = jnp.round(both[:, :DH] * (STEPS / largest)).astype(jnp.int32).astype(jnp.int16)
        step = largest * (1.0 / STEPS) / totals
        log_total = highest + jnp.log2(totals)
        log_rows = to_row(log_total.reshape(GROUP, SIZES[ch], DH))
        step_rows = to_row(step.reshape(GROUP, SIZES[ch], DH))
        zi = kv // 2
        for i in range(GROUP):
            xx, core = (kv % 2) * 2 + i // 4, (i % 4) // 2
            part = partial[i * SIZES[ch] : (i + 1) * SIZES[ch]]
            if i % 2 == 0:
                place, to, box, stats, count = zi * 2 + core, xx, ca, sa, 4
            else:
                place, to, box, stats, count = xx * 2 + core, zi, cb, sb, 8
            box[to, rows_of(ch), place * DH : (place + 1) * DH] = part
            stats[ch, to, place : place + 1] = log_rows[i : i + 1]
            stats[ch, to, count + place : count + place + 1] = step_rows[i : i + 1]

    merger = c == z // 2

    def act_start(condition, copy):
        if condition is True:
            copy.start()
        else:
            @pl.when(condition)
            def _():
                copy.start()

    def send_or_keep(here, pairs):
        for src, dst, send, recv, to in pairs:
            act_start(jnp.logical_not(here), remote(src, dst, send, recv, to))

        @pl.when(here)
        def _():
            for src, dst, *_ in pairs:
                dst[...] = src[...]

    def push_x(ch, xx):
        to, rows = device(z, xx, c), rows_of(ch)
        send_or_keep(
            xx == x,
            [
                (ca.at[xx, rows], ga.at[x, rows], first_send.at[0], first_recv.at[ch, 0], to),
                (sa.at[ch, xx], gsa.at[ch, x], first_send.at[1], first_recv.at[ch, 1], to),
            ],
        )

    def push_z(ch, zi):
        to, rows = device(2 * c + zi, x, c), rows_of(ch)
        send_or_keep(
            2 * c + zi == z,
            [
                (cb.at[zi, rows], gb.at[z, rows], first_send.at[2], first_recv.at[ch, 2], to),
                (sb.at[ch, zi], gsb.at[ch, z], first_send.at[3], first_recv.at[ch, 3], to),
            ],
        )

    def compute(ch):
        s = scores(ch, 0)
        for kv in range(KV_HALF):
            later = scores(ch, kv + 1) if kv + 1 < KV_HALF else None
            attend(ch, kv, s)
            s = later
            if kv in EARLY[ch]:
                push(ch, kv)
        for kv in range(KV_HALF):
            if kv not in EARLY[ch]:
                push(ch, kv)

    def push(ch, kv):
        if kv == 1:
            push_z(ch, 0)
        if kv == 2:
            push_x(ch, 0)
            push_x(ch, 1)
        if kv == 3:
            push_x(ch, 2)
            push_x(ch, 3)
            push_z(ch, 1)

    def weigh(parts):
        top = functools.reduce(jnp.maximum, parts)
        factors = [jnp.exp2(part - top) for part in parts]
        total = functools.reduce(jnp.add, factors)
        return [factor / total for factor in factors], top + jnp.log2(total)

    def merge_side(ch, count, got, stats, done):
        tiles = [stats[ch, i] for i in range(SIDE)]
        factors, logs = weigh([tile[:count] for tile in tiles])
        scales = [factors[i] * tiles[i][count : 2 * count] for i in range(SIDE)]
        for head in range(count):
            cols = slice(head * DH, (head + 1) * DH)
            added = functools.reduce(
                jnp.add,
                [
                    to_column(scales[i][head : head + 1], SIZES[ch]) * got[i, rows_of(ch), cols].astype(jnp.int32).astype(jnp.float32)
                    for i in range(SIDE)
                ],
            )
            done[head, boxed(ch)] = jnp.concatenate([added, jnp.broadcast_to(logs[head : head + 1], (8, 128))], axis=0)

    def merge(ch):
        wait(ga.at[0 : SIDE - 1, rows_of(ch)], first_recv.at[ch, 0])
        wait(gsa.at[ch, 0 : SIDE - 1], first_recv.at[ch, 1])
        merge_side(ch, 4, ga, gsa, da)
        for place in range(4):
            zz, core = 2 * c + place // 2, place % 2
            here = jnp.logical_and(zz == z, core == c)
            act_start(
                jnp.logical_not(here),
                remote(
                    da.at[place, boxed(ch)], ha.at[z, boxed(ch)], second_send.at[0], second_recv.at[ch, 0], device(zz, x, core)
                ),
            )

            @pl.when(here)
            def _():
                ha[z, boxed(ch)] = da[place, boxed(ch)]

        @pl.when(merger)
        def _():
            wait(gb.at[0 : SIDE - 1, rows_of(ch)], first_recv.at[ch, 2])
            wait(gsb.at[ch, 0 : SIDE - 1], first_recv.at[ch, 3])
            merge_side(ch, 8, gb, gsb, db)
            for place in range(8):
                xx, core = place // 2, place % 2
                here = jnp.logical_and(xx == x, core == c)
                act_start(
                    jnp.logical_not(here),
                    remote(
                        db.at[place, boxed(ch)], hb.at[x, boxed(ch)], second_send.at[1], second_recv.at[ch, 1], device(z, xx, core)
                    ),
                )

                @pl.when(here)
                def _():
                    hb[x, boxed(ch)] = db[place, boxed(ch)]

    def finish(ch):
        for side, got in ((0, ha), (1, hb)):
            @pl.when(merger)
            def _():
                wait(got.at[0 : SIDE - 1, boxed(ch)], second_recv.at[ch, side])

            @pl.when(jnp.logical_not(merger))
            def _():
                wait(got.at[:, boxed(ch)], second_recv.at[ch, side])

            size, first = SIZES[ch], STARTS[ch] + 8 * ch
            factors, _ = weigh([got[i, first + size : first + size + 1] for i in range(SIDE)])
            added = functools.reduce(
                jnp.add, [to_column(factors[i], size) * got[i, first : first + size] for i in range(SIDE)]
            )
            out_ref[rows_of(ch), side * DH : (side + 1) * DH] = added.astype(jnp.bfloat16)

    steps = {
        "offer": offer, "keys": keys_arrive, "prepare": prepare, "across": across, "gather": gather,
        "arrive": lambda ch: spread_wait(ch, 2), "compute": compute,
        "merge": merge, "finish": finish,
    }
    for name, *at in ORDER:
        steps[name](*at)

    wait(cand.at[0], core_send)
    wait(lens.at[0], kv_send.at[0])
    wait(raw.at[0], kv_send.at[1])
    for stage in range(3):
        wait(r1.at[:, 0 : SIDE - 1], q_send.at[stage])
    wait(ga.at[0 : SIDE - 1], first_send.at[0])
    wait(gsa.at[:, 0 : SIDE - 1], first_send.at[1])

    @pl.when(merger)
    def _():
        wait(gb.at[0:1], first_send.at[2])
        wait(gsb.at[:, 0:1], first_send.at[3])
        wait(da.at[0:3], second_send.at[0])
        wait(db.at[0:7], second_send.at[1])

    @pl.when(jnp.logical_not(merger))
    def _():
        wait(gb.at[0:2], first_send.at[2])
        wait(gsb.at[:, 0:2], first_send.at[3])
        wait(da, second_send.at[0])


def on_device(queries, keys, values, lengths, owner):
    vmem, dma = pltpu.VMEM, pltpu.SemaphoreType.DMA
    any_space = pl.BlockSpec(memory_space=pl.ANY)
    smem = pl.BlockSpec(memory_space=pltpu.SMEM)
    bf16, f32, i16 = jnp.bfloat16, jnp.float32, jnp.int16
    return pl.pallas_call(
        kernel,
        out_shape=jax.ShapeDtypeStruct((Q, 2 * DH), bf16),
        in_specs=[smem, smem, any_space, any_space, any_space],
        out_specs=pl.BlockSpec(memory_space=vmem),
        scratch_shapes=[
            vmem((2, Q, HALF), bf16),
            vmem((Q, HALF), bf16),
            vmem((2, SIDE, Q, QUARTER), bf16),
            vmem((2, SIDE, Q, QUARTER), bf16),
            vmem((Q, HALF), bf16),
            vmem((2, 2, BLK, KV_HALF * DH), bf16),
            vmem((2, 8, 128), jnp.int32),
            vmem((KV_HALF, 2 * DH, 2 * BLK), bf16),
            vmem((KV_HALF, 2 * BLK, 2 * DH), bf16),
            vmem((SIDE, Q, 4 * DH), i16),
            vmem((CHUNKS, SIDE, 8, 128), f32),
            vmem((2, Q, 8 * DH), i16),
            vmem((CHUNKS, 2, 16, 128), f32),
            vmem((SIDE, Q, 4 * DH), i16),
            vmem((CHUNKS, SIDE, 8, 128), f32),
            vmem((SIDE, Q, 8 * DH), i16),
            vmem((CHUNKS, SIDE, 16, 128), f32),
            vmem((4, Q + 8 * CHUNKS, DH), f32),
            vmem((8, Q + 8 * CHUNKS, DH), f32),
            vmem((SIDE, Q + 8 * CHUNKS, DH), f32),
            vmem((SIDE, Q + 8 * CHUNKS, DH), f32),
            dma, dma((CHUNKS,)),
            dma((2,)), dma((2,)),
            dma((CHUNKS + 2,)),
            dma((3,)), dma((CHUNKS, 3)),
            dma((4,)), dma((CHUNKS, 4)),
            dma((2,)), dma((CHUNKS, 2)),
        ],
        compiler_params=pltpu.CompilerParams(
            collective_id=0, has_side_effects=True, vmem_limit_bytes=56 * 2**20
        ),
        cost_estimate=pl.CostEstimate(
            flops=4 * H * Q * BLK * DH, bytes_accessed=6 * 2**20, transcendentals=H * Q * BLK
        ),
    )(lengths, owner, queries, keys, values)


def solution(mesh):
    in_specs = (
        P(("req", "ctx"), None),
        P(("req", "ctx"), None),
        P(("req", "ctx"), None),
        P(("req", "ctx")),
        P("req"),
    )
    return jax.shard_map(
        on_device, mesh=mesh, in_specs=in_specs, out_specs=P("req", "ctx"), check_vma=False
    )
```
